512 devices in a mesh: pipe: 16 (over z), tp: 32 (over x, y, core).
Axes of the slice: x: 4, y: 4, z: 16, core: 2. Of those that a mesh axis runs over, the one named last changes fastest.
Arguments:
- stream: bfloat16 [16, 2048, 4096], P('pipe', None, 'tp')
- incoming: bfloat16 [1, 2048, 4096], P(None, None, 'tp')
- chosen: int32 [16, 2, 512], P('pipe'), may hold values from 0 to 2047, as said below
- live: int32 [16, 2], P('pipe'), may hold values from 256 to 512, as said below
- norm_gain: float32 [16, 4096], P('pipe'), may hold values from 0.1 to 1.9
- router: bfloat16 [16, 4096], P('pipe'), may hold values from -0.09375 to 0.09375
- wq: bfloat16 [16, 4096, 4096], P('pipe', None, 'tp')
- wk: bfloat16 [16, 4096, 1024], P('pipe', None, 'tp')
- wv: bfloat16 [16, 4096, 1024], P('pipe', None, 'tp'), may hold values from -0.09375 to 0.09375
- wo: bfloat16 [16, 4096, 4096], P('pipe', None, 'tp'), may hold values from -0.09375 to 0.09375
Outputs:
- advanced: bfloat16 [16, 2048, 4096], P('pipe', None, 'tp')
The draws below stay inside these ranges and needn't reach their ends.
Inputs may be any that keep to these rules, and one draw needn't show every extreme that they name: `chosen`: each list holds 512 distinct token positions in increasing order. `live`: at every tick some section's list is full.
All inputs are finite; a program needn't handle non-finite values.
Results may differ from the reference program's by a relative error of at most 0.0025.
Values may be sent and summed in bfloat16 or wider, within the bound.
A program may use at most 64 MiB of HBM per device.

```python
import math
import jax
import jax.numpy as jnp
from jax import lax

D = 4096
HEADS = 32
KVH = 8
HD = 128
TOKENS = 2048
CAP = 512
TICKS = 2
N_PIPE = 16


def drawn_rows(key, lead):
    return jax.random.normal(key, (lead, TOKENS, D), jnp.float32)


def draw_stream(key, part):
    key = jax.random.fold_in(key, 3)
    return drawn_rows(key, N_PIPE).astype(jnp.bfloat16)


def draw_incoming(key, part):
    key = jax.random.fold_in(key, 5)
    return drawn_rows(key, TICKS - 1).astype(jnp.bfloat16)


def draw_chosen(key, part):
    key = jax.random.fold_in(key, 7)
    keys = jax.random.split(key, N_PIPE * TICKS)
    picks = jax.vmap(lambda one: jax.random.permutation(one, TOKENS)[:CAP])(keys)
    return jnp.sort(picks, axis=-1).reshape(N_PIPE, TICKS, CAP).astype(jnp.int32)


def draw_live(key, part):
    key = jax.random.fold_in(key, 9)
    first, second = jax.random.split(key)
    counts = jax.random.randint(first, (N_PIPE, TICKS), CAP // 2, CAP + 1)
    full = jax.random.randint(second, (TICKS,), 0, N_PIPE)
    sections = jnp.arange(N_PIPE)[:, None]
    return jnp.where(sections == full[None, :], CAP, counts).astype(jnp.int32)


def query_base(key):
    return jax.random.normal(key, (N_PIPE, D, HEADS * HD), jnp.float32)


def draw_wq(key, part):
    return (query_base(key) * D ** (-0.5)).astype(jnp.bfloat16)


def draw_wk(key, part):
    key = jax.random.fold_in(key, 11)
    first = jax.random.fold_in(key, 0)
    return (jax.random.normal(first, (N_PIPE, D, KVH * HD), jnp.float32) * D ** (-0.5)).astype(jnp.bfloat16)


def levels(stream_key, dims, cuts, least, high):
    def one(dim, shards_of):
        draws = jax.random.uniform(jax.random.fold_in(jax.random.fold_in(stream_key, 6), dim), (shards_of,), jnp.float32, least / len(cuts), high / len(cuts))
        return jnp.repeat(jnp.exp(draws), dims[dim] // shards_of).reshape((-1,) + (1,) * (len(dims) - dim - 1))

    loudness = one(*cuts[0])
    for cut in cuts[1:]:
        loudness = loudness * one(*cut)
    return loudness


def scatter_about(stream_key, dims, spread, reach, pieces=(), held_as=jnp.bfloat16):
    factor_of = levels(stream_key, dims, pieces, -0.22, 0.18) if pieces else 1.0
    drawn = jax.random.normal(stream_key, dims, jnp.float32) * spread * factor_of
    return jnp.minimum(jnp.maximum(drawn, -reach), reach).astype(held_as)


def setup_inputs(seed: int = 0) -> dict:
    streams_of = jax.random.split(jax.random.key(seed), 11)
    stream = draw_stream(jax.random.fold_in(streams_of[10], 71), 0)
    incoming = draw_incoming(jax.random.fold_in(streams_of[10], 71), 0)
    chosen = draw_chosen(jax.random.fold_in(streams_of[10], 71), 0)
    live = draw_live(jax.random.fold_in(streams_of[10], 71), 0)
    norm_gain = jnp.clip(1.0 + 0.18 * jax.random.normal(streams_of[4], (N_PIPE, D), jnp.float32), 0.1, 1.9)
    router = scatter_about(streams_of[5], (N_PIPE, D), D ** -0.5, 0.09375, ((0, 16),))
    wq = draw_wq(jax.random.fold_in(streams_of[10], 71), 0)
    wk = draw_wk(jax.random.fold_in(streams_of[10], 71), 0)
    wv = scatter_about(streams_of[8], (N_PIPE, D, KVH * HD), D ** -0.5, 0.09375, ((0, 16), (2, 32)))
    wo = scatter_about(streams_of[9], (N_PIPE, HEADS * HD, D), (HEADS * HD) ** -0.5, 0.09375, ((0, 16), (2, 32)))
    return {"stream": stream, "incoming": incoming, "chosen": chosen, "live": live, "norm_gain": norm_gain, "router": router, "wq": wq, "wk": wk, "wv": wv, "wo": wo}


def rotate(values, position):
    half = values.shape[-1] // 2
    freq = jnp.exp(-math.log(500000.0) * 2.0 * jnp.arange(half, dtype=jnp.float32) / values.shape[-1])
    angle = position[:, None] * freq[None, :]
    cosine = jnp.cos(angle)[:, None, :]
    sine = jnp.sin(angle)[:, None, :]
    first = values[..., :half]
    second = values[..., half:]
    return jnp.concatenate([first * cosine - second * sine, second * cosine + first * sine], axis=-1)

def routed(state, index, count, gain, route, wq, wk, wv, wo):
    index = index.astype(jnp.int32)
    picked = jnp.take(state, index, axis=0)
    width = picked.astype(jnp.float32)
    cap = picked.shape[0]
    rstd = lax.rsqrt(lax.optimization_barrier(jnp.mean(width * width, axis=1)) + 1e-05)
    scaled = (width * gain).astype(jnp.bfloat16)
    position = index.astype(jnp.float32)
    logit = jnp.dot(scaled, route, preferred_element_type=jnp.float32) * rstd
    query = jnp.dot(scaled, wq, preferred_element_type=jnp.float32) * rstd[:, None]
    query = rotate(query.reshape(cap, HEADS, HD), position).astype(jnp.bfloat16)
    key_lin = (jnp.dot(scaled, wk, preferred_element_type=jnp.float32) * rstd[:, None]).astype(jnp.bfloat16)
    keys = rotate(key_lin.reshape(cap, KVH, HD).astype(jnp.float32), position).astype(jnp.bfloat16)
    values = (jnp.dot(scaled, wv, preferred_element_type=jnp.float32) * rstd[:, None]).astype(jnp.bfloat16)
    values = values.reshape(cap, KVH, HD)
    grouped = query.reshape(cap, KVH, HEADS // KVH, HD)
    scores = jnp.einsum('qgrd,kgd->grqk', grouped.astype(jnp.float32), keys.astype(jnp.float32)) / math.sqrt(HD)
    slots = jnp.arange(cap)
    allowed = (slots[None, :] <= slots[:, None]) & (slots[None, :] < count)
    scores = jnp.where(allowed, scores, -jnp.inf)
    top = lax.optimization_barrier(jnp.max(scores, axis=-1, keepdims=True))
    weights = jnp.exp(scores - top)
    probs = (weights / lax.optimization_barrier(jnp.sum(weights, axis=-1, keepdims=True))).astype(jnp.bfloat16)
    attended = jnp.einsum('grqk,kgd->qgrd', probs.astype(jnp.float32), values.astype(jnp.float32))
    attended = attended.astype(jnp.bfloat16).reshape(cap, HEADS * HD)
    delta = jnp.dot(attended, wo, preferred_element_type=jnp.float32)
    mixing = jax.nn.sigmoid(logit) * (slots < count).astype(jnp.float32)
    updated = (width + mixing[:, None] * delta).astype(jnp.bfloat16)
    return state.at[index].set(updated)

def reference(stream, incoming, chosen, live, norm_gain, router, wq, wk, wv, wo):
    sections = stream.shape[0]

    def apply(block, state, tick):
        return routed(state, chosen[block, tick], live[block, tick], norm_gain[block], router[block], wq[block], wk[block], wv[block], wo[block])
    states = [apply(block, stream[block], 0) for block in range(sections)]
    for tick in range(1, TICKS):
        states = [apply(0, incoming[tick - 1], tick)] + [apply(block, states[block - 1], tick) for block in range(1, sections)]
    return jnp.stack(states)
```

```python
import functools
import math

import jax
import jax.numpy as jnp
import numpy as np
from jax import lax
from jax.experimental import pallas as pl
from jax.experimental.pallas import tpu as pltpu
from jax.sharding import PartitionSpec as P

MESH = pl.DeviceIdType.MESH
F32 = jnp.float32
BF16 = jnp.bfloat16

D = 4096
TOKENS = 2048
CAP = 512
HD = 128
N = 4
R = CAP // N
H = R // 2


def kernel(
    stream, incoming, chosen, live, gain, router, freq, wq, wk, wv, wo, out,
    strm, inc, bulk, wqa, woa, wkl, wvl, w2o, w2p, w2, lprev, lsp, cosb, sinb, gath, pst, bp, kvb, kc, vc,
    qs, accq, acck, ssb, lgb, mixb, accd, ub, u0, u1s, u1, mt, facc,
    loc, ag_s, ag_r, pk_s, pk_r, kv_s, kv_r, uz_s, uz_r, wx_s, wx_r, e_s, e_r,
):
    z = lax.axis_index("pipe")
    t = lax.axis_index("tp")
    nz = lax.axis_size("pipe")
    c = t % 2
    chip = t // 2
    y = chip % 4
    x = chip // 4
    p = x * (1 - c) + y * c
    q = y * (1 - c) + x * c
    own = q * 4 + p
    partner = (z, chip * 2 + 1 - c)
    par = y % 2
    twin = x * 4 + y + 1 - 2 * par

    def dev(pp, qq):
        xx = pp * (1 - c) + qq * c
        yy = qq * (1 - c) + pp * c
        return (z, (xx * 4 + yy) * 2 + c)

    znext = (z + 1) % nz
    zprev = (z + nz - 1) % nz
    other = chip * 2 + 1 - c

    barrier = pltpu.get_barrier_semaphore()
    peers = [dev((p + d) % 4, q) for d in (1, 2, 3)] + [dev(p, (q + d) % 4) for d in (1, 2, 3)]
    peers += [partner, (z, twin * 2 + 1 - c)]
    peers += [(znext, t), (znext, other), (zprev, t), (zprev, other)]
    for peer in peers:
        pl.semaphore_signal(barrier, inc=1, device_id=peer, device_id_type=MESH)

    sends = []

    def put(src, dst, s_sem, r_sem, device):
        cp = pltpu.make_async_remote_copy(
            src_ref=src, dst_ref=dst, send_sem=s_sem, recv_sem=r_sem, device_id=device, device_id_type=MESH
        )
        cp.start()
        sends.append(cp)

    def got(dst, s_sem, r_sem):
        pltpu.make_async_remote_copy(
            src_ref=dst, dst_ref=dst, send_sem=s_sem, recv_sem=r_sem, device_id=partner, device_id_type=MESH
        ).wait_recv()

    mycols = pl.ds(pl.multiple_of(c * 128, 128), 128)

    def local(k, src, dst):
        cp = pltpu.make_async_copy(src, dst, loc.at[k])
        cp.start()
        return cp

    cp_strm = local(0, stream, strm)
    cp_wk = local(1, wk, wkl)
    cp_wv = local(2, wv, wvl)
    cp_wq = local(3, wq, wqa.at[:, mycols])
    cp_wo = local(4, wo, woa.at[:, mycols])
    cp_inc = local(5, incoming, inc)

    zf = jnp.minimum(z, 1).astype(F32)
    cf = c.astype(F32)

    def rows(g):
        return pl.ds(pl.multiple_of(g * R + c * H, H), H)

    def other_rows(g):
        return pl.ds(pl.multiple_of(g * R + (1 - c) * H, H), H)

    def spread(tick):
        row = chosen[tick : tick + 1, :].astype(F32)
        for k in range(CAP // 128):
            lsp[tick, k * 128 : (k + 1) * 128, :] = jnp.transpose(
                jnp.broadcast_to(row[:, k * 128 : (k + 1) * 128], (128, 128))
            )

    def take_rows(tick, g, source):
        lane = lax.broadcasted_iota(jnp.int32, (R, 256), 1).astype(F32)
        pos = lsp[tick, g * R : (g + 1) * R, :]
        pos = jnp.concatenate([pos, pos], axis=1)
        total = jnp.zeros((R, 128), F32)
        for k in range(TOKENS // 256):
            hot = jnp.where(pos == lane + float(k * 256), 1.0, 0.0).astype(BF16)
            total += jnp.dot(hot, source(k), preferred_element_type=F32)
        return total

    def mine_of(value):
        low, high = value[:H], value[H:]
        return (low * (1 - cf) + high * cf).astype(BF16), (high * (1 - cf) + low * cf).astype(BF16)

    spread(0)
    cp_strm.wait()
    for g in range(N):
        mine, others = mine_of(take_rows(0, g, lambda k: strm[k * 256 : (k + 1) * 256, :]))
        gath[0, g, own, :, mycols] = mine
        pst[0, g] = others
    pl.semaphore_wait(barrier, len(peers))
    for g in range(N):
        put(pst.at[0, g], gath.at[0, g, p * 4 + q, :, mycols], pk_s.at[0, g], pk_r.at[0, g], partner)

    def gather_own(a, g):
        for k, d in enumerate((1, 3, 2)):
            put(gath.at[a, g, own], gath.at[a, g, own], ag_s.at[a, g, k], ag_r.at[a, g, k], dev((p + d) % 4, q))

    def group(qq):
        return pl.ds(qq * 4, 4)

    def gather_group(a, g):
        for k, d in enumerate((1, 3, 2)):
            got(gath.at[a, g, q * 4 + (p + 4 - d) % 4], ag_s.at[a, g, k], ag_r.at[a, g, k])
        for k, d in ((3, 1), (4, 3)):
            mine = gath.at[a, g, group(q)]
            put(mine, mine, ag_s.at[a, g, k], ag_r.at[a, g, k], dev(p, (q + d) % 4))

    def gather_far(a, g):
        before = (q + 3) % 4
        after = (q + 1) % 4
        got(gath.at[a, g, group(before)], ag_s.at[a, g, 3], ag_r.at[a, g, 3])
        half = gath.at[a, g, pl.ds(before * 4, 2)]
        put(half, half, ag_s.at[a, g, 5], ag_r.at[a, g, 5], dev(p, after))
        got(gath.at[a, g, group(after)], ag_s.at[a, g, 4], ag_r.at[a, g, 4])
        half = gath.at[a, g, pl.ds(after * 4 + 2, 2)]
        put(half, half, ag_s.at[a, g, 6], ag_r.at[a, g, 6], dev(p, before))

    def gather_end(a, g):
        far = (q + 2) % 4
        got(gath.at[a, g, pl.ds(far * 4, 2)], ag_s.at[a, g, 5], ag_r.at[a, g, 5])
        got(gath.at[a, g, pl.ds(far * 4 + 2, 2)], ag_s.at[a, g, 6], ag_r.at[a, g, 6])

    def features(qq, pp):
        return (pp * 4 + qq) * (1 - c) + (qq * 4 + pp) * c

    def project(tick, g, shift, first):
        qq = (q + shift) % 4
        query = jnp.zeros((H, 256), F32) if first else accq[g]
        keyval = jnp.zeros((H, 128), F32) if first else acck[g]
        square = jnp.zeros((H, 128), F32) if first else ssb[g]
        logit = jnp.zeros((H, 128), F32) if first else lgb[g]
        for pp in range(4):
            at = pl.ds(pl.multiple_of(features(qq, pp) * 256, 256), 256)
            wide = gath[2 * tick, g, qq * 4 + pp].astype(F32)
            scaled = (wide * gain[:, at]).astype(BF16)
            two = wide * wide
            square += two[:, :128] + two[:, 128:]
            two = scaled.astype(F32) * router[:, at].astype(F32)
            logit += two[:, :128] + two[:, 128:]
            query += jnp.dot(scaled, wqa[at, :], preferred_element_type=F32)
            keyval += jnp.dot(scaled, w2[at, :], preferred_element_type=F32)
        accq[g] = query
        acck[g] = keyval
        ssb[g] = square
        lgb[g] = logit

    def rope(value, cosine, sine):
        return value * cosine + pltpu.roll(value, 64, 1) * sine

    def project_end(tick, g):
        rstd = lax.rsqrt(jnp.sum(ssb[g], axis=1, keepdims=True) / D + 1e-05)
        kv = (acck[g] * rstd).astype(BF16)
        kvb[tick, par, rows(g), :] = kv
        part = kvb.at[tick, par, rows(g), :]
        put(part, part, kv_s.at[tick, g, 0], kv_r.at[tick, g, 0], (z, twin * 2 + c))
        put(part, part, kv_s.at[tick, g, 1], kv_r.at[tick, g, 1], (z, twin * 2 + 1 - c))
        put(part, part, kv_s.at[tick, g, 2], kv_r.at[tick, g, 2], partner)
        cosine = cosb[tick, rows(g), :]
        sine = sinb[tick, rows(g), :]
        query = accq[g] * rstd
        qs[g, :H, :] = rope(query[:, :128], cosine, sine).astype(BF16)
        qs[g, H:, :] = rope(query[:, 128:], cosine, sine).astype(BF16)
        logit = jnp.sum(lgb[g], axis=1, keepdims=True) * rstd
        slot = lax.broadcasted_iota(jnp.int32, (H, 1), 0) + (g * R + c * H)
        alive = jnp.where(slot < live[:, tick : tick + 1], 1.0, 0.0)
        mixb[g] = jnp.broadcast_to(jax.nn.sigmoid(logit) * alive, (H, 128))

    def attend(tick, g):
        got(kvb.at[tick, 1 - par, rows(g), :], kv_s.at[tick, g, 0], kv_r.at[tick, g, 0])
        got(kvb.at[tick, 1 - par, other_rows(g), :], kv_s.at[tick, g, 1], kv_r.at[tick, g, 1])
        got(kvb.at[tick, par, other_rows(g), :], kv_s.at[tick, g, 2], kv_r.at[tick, g, 2])
        span = slice(g * R, (g + 1) * R)
        low = kvb[tick, 0, span, :].astype(F32)
        high = kvb[tick, 1, span, :].astype(F32)
        left = lax.broadcasted_iota(jnp.int32, (R, 128), 1) < 64
        key = jnp.where(left, low, pltpu.roll(high, 64, 1))
        kc[span, :] = rope(key, cosb[tick, span, :], sinb[tick, span, :]).astype(BF16)
        vc[span, :] = jnp.where(left, pltpu.roll(low, 64, 1), high).astype(BF16)
        upto = (g + 1) * R
        scores = lax.dot_general(
            qs[g], kc[:upto, :], (((1,), (1,)), ((), ())), preferred_element_type=F32
        ) * (1.0 / math.sqrt(HD))
        row = lax.broadcasted_iota(jnp.int32, (2 * H, upto), 0)
        row = jnp.where(row < H, row, row - H) + (g * R + c * H)
        col = lax.broadcasted_iota(jnp.int32, (2 * H, upto), 1)
        scores = jnp.where((col <= row) & (col < live[:, tick : tick + 1]), scores, -jnp.inf)
        top = jnp.max(scores, axis=1, keepdims=True)
        weights = jnp.exp(scores - top)
        probs = (weights / jnp.sum(weights, axis=1, keepdims=True)).astype(BF16)
        result = jnp.dot(probs, vc[:upto, :], preferred_element_type=F32).astype(BF16)
        a = 2 * tick + 1
        gath[a, g, own, :, 0:128] = result[:H]
        gath[a, g, own, :, 128:256] = result[H:]
        gather_own(a, g)

    def mix_out(tick, g, shift, first):
        qq = (q + shift) % 4
        total = jnp.zeros((H, 256), F32) if first else accd[g]
        for pp in range(4):
            at = pl.ds(pl.multiple_of(features(qq, pp) * 256, 256), 256)
            total += jnp.dot(gath[2 * tick + 1, g, qq * 4 + pp], woa[at, :], preferred_element_type=F32)
        accd[g] = total

    def updated(tick, g):
        mixing = jnp.concatenate([mixb[g], mixb[g]], axis=1)
        return (gath[2 * tick, g, own].astype(F32) + mixing * accd[g]).astype(BF16)

    def finish(tick, g):
        new = updated(tick, g)
        if tick == 0:
            ub[g] = new
            put(ub.at[g], u0.at[rows(g), :], uz_s.at[g, 0], uz_r.at[g, 0], (znext, t))
            put(ub.at[g], u0.at[rows(g), :], uz_s.at[g, 1], uz_r.at[g, 1], (znext, other))
        else:
            low, high = new[:, :128].astype(F32), new[:, 128:].astype(F32)
            u1s[g] = (high * (1 - cf) + low * cf).astype(BF16)
            put(u1s.at[g], u1.at[rows(g), :], e_s.at[g], e_r.at[g], partner)
            u1[rows(g), :] = (low * (1 - cf) + high * cf).astype(BF16)

    def tables(tick):
        for g in range(CAP // 128):
            span = slice(g * 128, (g + 1) * 128)
            angle = lsp[tick, span, :] * freq[...]
            sign = jnp.where(lax.broadcasted_iota(jnp.int32, (128, 128), 1) < 64, -1.0, 1.0)
            cosb[tick, span, :] = jnp.cos(angle)
            sinb[tick, span, :] = jnp.sin(angle) * sign

    def place_kv():
        cp_wk.wait()
        cp_wv.wait()
        row = lax.broadcasted_iota(jnp.int32, (32, 128), 0)
        col = lax.broadcasted_iota(jnp.int32, (32, 128), 1)
        hot_k = jnp.where(col == row + 32 * c, 1.0, 0.0).astype(BF16)
        hot_v = jnp.where(col == row + 64 + 32 * c, 1.0, 0.0).astype(BF16)

        def some(k, _):
            at = pl.ds(pl.multiple_of(k * 512, 512), 512)
            w2o[at, :] = (
                jnp.dot(wkl[at, :], hot_k, preferred_element_type=F32)
                + jnp.dot(wvl[at, :], hot_v, preferred_element_type=F32)
            ).astype(BF16)
            return 0

        lax.fori_loop(0, D // 512, some, 0)

    def join_kv():
        got(w2p, wx_s.at[1], wx_r.at[1])

        def some(k, _):
            at = pl.ds(pl.multiple_of(k * 512, 512), 512)
            w2[at, :] = w2o[at, :] + w2p[at, :]
            return 0

        lax.fori_loop(0, D // 512, some, 0)

    for g in range(N):
        got(gath.at[0, g, own, :, mycols], pk_s.at[0, g], pk_r.at[0, g])
        gather_own(0, g)
    put(wq, wqa.at[:, mycols], wx_s.at[0], wx_r.at[0], partner)
    place_kv()
    put(w2o, w2p, wx_s.at[1], wx_r.at[1], partner)
    put(chosen, lprev, wx_s.at[3], wx_r.at[3], (znext, t))
    put(stream, bulk, wx_s.at[4], wx_r.at[4], (znext, t))
    for g in range(N):
        gather_group(0, g)
    put(wo, woa.at[:, mycols], wx_s.at[2], wx_r.at[2], partner)
    gather_far(0, 0)
    tables(0)
    gather_far(0, 1)

    def ready_weights():
        cp_wq.wait()
        got(wqa.at[:, mycols], wx_s.at[0], wx_r.at[0])
        join_kv()

    def ready_wo():
        cp_wo.wait()
        got(woa.at[:, mycols], wx_s.at[2], wx_r.at[2])

    def near(tick, g):
        project(tick, g, 0, True)
        project(tick, g, 3, False)
        project(tick, g, 1, False)

    def rest(tick, g):
        gather_end(2 * tick, g)
        project(tick, g, 2, False)
        project_end(tick, g)

    def near_out(tick, g):
        mix_out(tick, g, 0, True)
        mix_out(tick, g, 3, False)
        mix_out(tick, g, 1, False)

    def rest_out(tick, g):
        gather_end(2 * tick + 1, g)
        mix_out(tick, g, 2, False)
        finish(tick, g)

    def token_map():
        row = chosen[1:2, :].astype(F32)

        def some(k, _):
            at = pl.ds(pl.multiple_of(k * 256, 256), 256)
            token = (lax.broadcasted_iota(jnp.int32, (256, CAP), 0) + k * 256).astype(F32)
            mt[at, :] = jnp.where(token == row, 1.0, 0.0).astype(BF16)
            return 0

        lax.fori_loop(0, TOKENS // 256, some, 0)

    def base_rows():
        cp_inc.wait()
        got(bulk, wx_s.at[4], wx_r.at[4])
        got(lprev, wx_s.at[3], wx_r.at[3])

        def some(k, _):
            at = pl.ds(pl.multiple_of(k * 256, 256), 256)
            bulk_rows = bulk[at, :].astype(F32) * zf + inc[at, :].astype(F32) * (1 - zf)
            strm[at, :] = bulk_rows.astype(BF16)
            return 0

        lax.fori_loop(0, TOKENS // 256, some, 0)

    def base_take(g):
        mine, others = mine_of(take_rows(1, g, lambda k: strm[k * 256 : (k + 1) * 256, :]))
        bp[g, :, mycols] = mine
        pst[1, g] = others
        put(pst.at[1, g], bp.at[g, :, mycols], pk_s.at[1, g], pk_r.at[1, g], partner)

    def previous():
        return lprev[0:1, :].astype(F32) * zf - (1 - zf)

    ready_weights()
    near(0, 0)
    gather_far(0, 2)
    rest(0, 0)
    near(0, 1)
    gather_far(0, 3)
    rest(0, 1)
    attend(0, 0)
    near(0, 2)
    rest(0, 2)
    attend(0, 1)
    gather_group(1, 0)
    near(0, 3)
    rest(0, 3)
    attend(0, 2)
    gather_group(1, 1)
    gather_far(1, 0)
    attend(0, 3)
    gather_group(1, 2)
    gather_far(1, 1)
    ready_wo()
    near_out(0, 0)
    gather_group(1, 3)
    gather_far(1, 2)
    rest_out(0, 0)
    near_out(0, 1)
    gather_far(1, 3)
    rest_out(0, 1)
    spread(1)
    base_rows()
    for g in range(N):
        base_take(g)
    near_out(0, 2)
    rest_out(0, 2)
    near_out(0, 3)
    rest_out(0, 3)
    tables(1)
    token_map()

    for g in range(N):
        got(bp.at[g, :, mycols], pk_s.at[1, g], pk_r.at[1, g])
    for g in range(N):
        got(u0.at[rows(g), :], uz_s.at[g, 0], uz_r.at[g, 0])
        got(u0.at[other_rows(g), :], uz_s.at[g, 1], uz_r.at[g, 1])
    for g in range(N):
        pos = lsp[1, rows(g), :]
        pos = jnp.concatenate([pos] * (CAP // 128), axis=1)
        same = jnp.where(pos == previous(), 1.0, 0.0)
        kept = 1.0 - jnp.sum(same, axis=1, keepdims=True)
        moved = jnp.dot(same.astype(BF16), u0[...], preferred_element_type=F32)
        gath[2, g, own] = (bp[g].astype(F32) * kept + moved).astype(BF16)
        gather_own(2, g)

    def unlisted():
        mine = u0[:, mycols]
        both = jnp.concatenate([mine, jnp.ones((CAP, 128), BF16)], axis=1)
        row = previous()

        def some(k, _):
            at = pl.ds(pl.multiple_of(k * 256, 256), 256)
            token = (lax.broadcasted_iota(jnp.int32, (256, CAP), 0) + k * 256).astype(F32)
            hot = jnp.where(token == row, 1.0, 0.0).astype(BF16)
            moved = jnp.dot(hot, both, preferred_element_type=F32)
            listed = jnp.dot(mt[at, :], jnp.ones((CAP, 128), BF16), preferred_element_type=F32)
            state = strm[at, :].astype(F32) * (1.0 - moved[:, 128:]) + moved[:, :128]
            facc[at, :] = state * (1.0 - listed)
            return 0

        lax.fori_loop(0, TOKENS // 256, some, 0)

    for g in range(N):
        gather_group(2, g)
    unlisted()
    gather_far(2, 0)
    gather_far(2, 1)
    near(1, 0)
    gather_far(2, 2)
    rest(1, 0)
    near(1, 1)
    gather_far(2, 3)
    rest(1, 1)
    attend(1, 0)
    near(1, 2)
    rest(1, 2)
    attend(1, 1)
    gather_group(3, 0)
    near(1, 3)
    rest(1, 3)
    attend(1, 2)
    gather_group(3, 1)
    gather_far(3, 0)
    attend(1, 3)
    gather_group(3, 2)
    gather_far(3, 1)
    near_out(1, 0)
    gather_group(3, 3)
    gather_far(3, 2)
    rest_out(1, 0)
    near_out(1, 1)
    gather_far(3, 3)
    rest_out(1, 1)
    near_out(1, 2)
    rest_out(1, 2)
    near_out(1, 3)
    rest_out(1, 3)
    for g in range(N):
        got(u1.at[other_rows(g), :], e_s.at[g], e_r.at[g])

    def write(k, _):
        at = pl.ds(pl.multiple_of(k * 256, 256), 256)
        new = jnp.dot(mt[at, :], u1[...], preferred_element_type=F32)
        out[at, :] = (facc[at, :] + new).astype(BF16)
        return 0

    lax.fori_loop(0, TOKENS // 256, write, 0)
    for cp in sends:
        cp.wait_send()


def body(stream, incoming, chosen, live, norm_gain, router, wq, wk, wv, wo):
    half = HD // 2
    freq = np.exp(-math.log(500000.0) * 2.0 * np.arange(half) / HD)
    freq = jnp.asarray(np.concatenate([freq, freq])[None, :], F32)
    vmem = pl.BlockSpec(memory_space=pltpu.VMEM)
    hbm = pl.BlockSpec(memory_space=pl.ANY)
    dma = pltpu.SemaphoreType.DMA
    scratch = [
        pltpu.VMEM((TOKENS, 128), BF16),
        pltpu.VMEM((TOKENS, 128), BF16),
        pltpu.VMEM((TOKENS, 128), BF16),
        pltpu.VMEM((D, 256), BF16),
        pltpu.VMEM((D, 256), BF16),
        pltpu.VMEM((D, 32), BF16),
        pltpu.VMEM((D, 32), BF16),
        pltpu.VMEM((D, 128), BF16),
        pltpu.VMEM((D, 128), BF16),
        pltpu.VMEM((D, 128), BF16),
        pltpu.VMEM((2, CAP), jnp.int32),
        pltpu.VMEM((2, CAP, 128), F32),
        pltpu.VMEM((2, CAP, 128), F32),
        pltpu.VMEM((2, CAP, 128), F32),
        pltpu.VMEM((4, N, 16, H, 256), BF16),
        pltpu.VMEM((2, N, H, 128), BF16),
        pltpu.VMEM((N, H, 256), BF16),
        pltpu.VMEM((2, 2, CAP, 128), BF16),
        pltpu.VMEM((CAP, 128), BF16),
        pltpu.VMEM((CAP, 128), BF16),
        pltpu.VMEM((N, 2 * H, 128), BF16),
        pltpu.VMEM((N, H, 256), F32),
        pltpu.VMEM((N, H, 128), F32),
        pltpu.VMEM((N, H, 128), F32),
        pltpu.VMEM((N, H, 128), F32),
        pltpu.VMEM((N, H, 128), F32),
        pltpu.VMEM((N, H, 256), F32),
        pltpu.VMEM((N, H, 256), BF16),
        pltpu.VMEM((CAP, 256), BF16),
        pltpu.VMEM((N, H, 128), BF16),
        pltpu.VMEM((CAP, 128), BF16),
        pltpu.VMEM((TOKENS, CAP), BF16),
        pltpu.VMEM((TOKENS, 128), F32),
        dma((6,)),
        dma((4, N, 7)),
        dma((4, N, 7)),
        dma((2, N)),
        dma((2, N)),
        dma((2, N, 3)),
        dma((2, N, 3)),
        dma((N, 2)),
        dma((N, 2)),
        dma((5,)),
        dma((5,)),
        dma((N,)),
        dma((N,)),
    ]
    result = pl.pallas_call(
        kernel,
        out_shape=jax.ShapeDtypeStruct((TOKENS, 128), BF16),
        in_specs=[hbm, hbm, vmem, vmem, vmem, vmem, vmem, hbm, hbm, hbm, hbm],
        out_specs=vmem,
        scratch_shapes=scratch,
        compiler_params=pltpu.CompilerParams(
            collective_id=0, has_side_effects=True, vmem_limit_bytes=48 * 2**20
        ),
        name="relay",
    )(stream[0], incoming[0], chosen[0], live, norm_gain, router, freq, wq[0], wk[0], wv[0], wo[0])
    return result[None]


def solution(mesh):
    in_specs = (
        P("pipe", None, "tp"),
        P(None, None, "tp"),
        P("pipe", None, None),
        P("pipe", None),
        P("pipe", None),
        P("pipe", None),
        P("pipe", None, "tp"),
        P("pipe", None, "tp"),
        P("pipe", None, "tp"),
        P("pipe", None, "tp"),
    )
    out_specs = P("pipe", None, "tp")
    return jax.shard_map(body, mesh=mesh, in_specs=in_specs, out_specs=out_specs, check_vma=False)
```

```python
import functools
import math

import jax
import jax.numpy as jnp
import numpy as np
from jax import lax
from jax.experimental import pallas as pl
from jax.experimental.pallas import tpu as pltpu
from jax.sharding import PartitionSpec as P

MESH = pl.DeviceIdType.MESH
F32 = jnp.float32
BF16 = jnp.bfloat16

D = 4096
TOKENS = 2048
CAP = 512
HD = 128
N = 2
R = CAP // N
H = R // 2


def kernel(
    stream, incoming, chosen, live, gain, router, freq, wq, wk, wv, wo, out,
    strm, inc, bulk, wall, woa, wod, wkl, wvl, w2o, w2p, gains, routes, same, lprev, lsp, cosb, sinb, gath, att, rss, rsr, pst, bp, kvb, kc, vc,
    qs, accp, ssb, lgb, mixb, accd, ub, accm, u0, u1s, u1, mt, facc,
    loc, ag_s, ag_r, at_s, at_r, rs_s, rs_r, wo_s, wo_r, pk_s, pk_r, kv_s, kv_r, uz_s, uz_r, wx_s, wx_r, e_s, e_r,
):
    z = lax.axis_index("pipe")
    t = lax.axis_index("tp")
    nz = lax.axis_size("pipe")
    c = t % 2
    chip = t // 2
    y = chip % 4
    x = chip // 4
    p = x * (1 - c) + y * c
    q = y * (1 - c) + x * c
    own = q * 4 + p
    partner = (z, chip * 2 + 1 - c)
    par = y % 2
    twin = x * 4 + y + 1 - 2 * par

    def dev(pp, qq):
        xx = pp * (1 - c) + qq * c
        yy = qq * (1 - c) + pp * c
        return (z, (xx * 4 + yy) * 2 + c)

    def cross(pp, qq):
        xx = pp * (1 - c) + qq * c
        yy = qq * (1 - c) + pp * c
        return (z, (xx * 4 + yy) * 2 + 1 - c)

    znext = (z + 1) % nz
    zprev = (z + nz - 1) % nz
    other = chip * 2 + 1 - c

    barrier = pltpu.get_barrier_semaphore()
    peers = [dev((p + d) % 4, q) for d in (1, 2, 3)] + [dev(p, (q + d) % 4) for d in (1, 2, 3)]
    peers += [cross((p + d) % 4, q) for d in (1, 2, 3)] + [cross(p, (q + d) % 4) for d in (1, 2, 3)] + [partner]
    peers += [(znext, t), (znext, other), (zprev, t), (zprev, other)]
    for peer in peers:
        pl.semaphore_signal(barrier, inc=1, device_id=peer, device_id_type=MESH)

    sends = []

    def put(src, dst, s_sem, r_sem, device):
        cp = pltpu.make_async_remote_copy(
            src_ref=src, dst_ref=dst, send_sem=s_sem, recv_sem=r_sem, device_id=device, device_id_type=MESH
        )
        cp.start()
        sends.append(cp)

    def got(dst, s_sem, r_sem):
        pltpu.make_async_remote_copy(
            src_ref=dst, dst_ref=dst, send_sem=s_sem, recv_sem=r_sem, device_id=partner, device_id_type=MESH
        ).wait_recv()

    mycols = pl.ds(pl.multiple_of(c * 128, 128), 128)

    def local(k, src, dst):
        cp = pltpu.make_async_copy(src, dst, loc.at[k])
        cp.start()
        return cp

    cp_strm = local(0, stream, strm)
    cp_wk = local(1, wk, wkl)
    cp_wv = local(2, wv, wvl)
    cp_inc = local(5, incoming, inc)

    def slot_of(k, cc):
        return ((k % 4) * 4 + k // 4) * (1 - cc) + k * cc

    def part(k):
        return pl.ds(pl.multiple_of(k * 256, 256), 256)

    def lay_out(source, target, sem):
        def some(k, _):
            pltpu.make_async_copy(source.at[part(k), :], target.at[part(slot_of(k, c)), mycols], sem).start()
            return 0

        lax.fori_loop(0, 16, some, 0)

    lay_out(wq, wall, loc.at[3])

    def put_out(source, target, columns, k):
        def some(i, _):
            pltpu.make_async_remote_copy(
                src_ref=source.at[part(i), :], dst_ref=target.at[part(slot_of(i, 1 - c)), columns],
                send_sem=wx_s.at[k], recv_sem=wx_r.at[k], device_id=partner, device_id_type=MESH,
            ).start()
            return 0

        lax.fori_loop(0, 16, some, 0)
        whole = target.at[:, columns]
        sends.append(
            pltpu.make_async_remote_copy(
                src_ref=whole, dst_ref=whole, send_sem=wx_s.at[k], recv_sem=wx_r.at[k],
                device_id=partner, device_id_type=MESH,
            )
        )

    def chip_of(pp, qq, cc):
        return (pp * 4 + qq) * (1 - cc) + (qq * 4 + pp) * cc

    def out_weights(d):
        qq = (q + d) % 4
        pp = (p + d) % 4
        for k in range(4):
            if d == 0:
                pltpu.make_async_copy(wo.at[part(chip_of(k, qq, c)), :], wod.at[q, k, :, mycols], loc.at[6]).start()
            else:
                pltpu.make_async_remote_copy(
                    src_ref=wo.at[part(chip_of(k, qq, c)), :], dst_ref=wod.at[q, k, :, mycols],
                    send_sem=wo_s.at[d, 0], recv_sem=wo_r.at[d, 0], device_id=dev(p, qq), device_id_type=MESH,
                ).start()
            pltpu.make_async_remote_copy(
                src_ref=wo.at[part(chip_of(k, pp, 1 - c)), :], dst_ref=wod.at[p, k, :, mycols],
                send_sem=wo_s.at[d, 1], recv_sem=wo_r.at[d, 1], device_id=cross(pp, q), device_id_type=MESH,
            ).start()
        for way in range(2):
            if d or way:
                whole = wod.at[0, :, :, mycols]
                sends.append(
                    pltpu.make_async_remote_copy(
                        src_ref=whole, dst_ref=whole, send_sem=wo_s.at[d, way], recv_sem=wo_r.at[d, way],
                        device_id=partner, device_id_type=MESH,
                    )
                )

    theircols = pl.ds(pl.multiple_of((1 - c) * 128, 128), 128)
    zf = jnp.minimum(z, 1).astype(F32)
    cf = c.astype(F32)

    def rows(g):
        return pl.ds(pl.multiple_of(g * R + c * H, H), H)

    def other_rows(g):
        return pl.ds(pl.multiple_of(g * R + (1 - c) * H, H), H)

    def spread(tick):
        row = chosen[tick : tick + 1, :].astype(F32)
        for k in range(CAP // 128):
            lsp[tick, k * 128 : (k + 1) * 128, :] = jnp.transpose(
                jnp.broadcast_to(row[:, k * 128 : (k + 1) * 128], (128, 128))
            )

    def take_rows(tick, g, source):
        lane = lax.broadcasted_iota(jnp.int32, (R, 256), 1).astype(F32)
        pos = lsp[tick, g * R : (g + 1) * R, :]
        pos = jnp.concatenate([pos, pos], axis=1)
        total = jnp.zeros((R, 128), F32)
        for k in range(TOKENS // 256):
            hot = jnp.where(pos == lane + float(k * 256), 1.0, 0.0).astype(BF16)
            total += jnp.dot(hot, source(k), preferred_element_type=F32)
        return total

    def mine_of(value):
        low, high = value[:H], value[H:]
        return (low * (1 - cf) + high * cf).astype(BF16), (high * (1 - cf) + low * cf).astype(BF16)

    def gather_own(a, g):
        for k, d in enumerate((1, 3, 2)):
            put(gath.at[a, g, own], gath.at[a, g, own], ag_s.at[a, g, k], ag_r.at[a, g, k], dev((p + d) % 4, q))

    def group(qq):
        return pl.ds(qq * 4, 4)

    def gather_group(a, g):
        for k, d in enumerate((1, 3, 2)):
            got(gath.at[a, g, q * 4 + (p + 4 - d) % 4], ag_s.at[a, g, k], ag_r.at[a, g, k])
        for k, d in ((3, 1), (4, 3)):
            mine = gath.at[a, g, group(q)]
            put(mine, mine, ag_s.at[a, g, k], ag_r.at[a, g, k], dev(p, (q + d) % 4))

    def gather_far(a, g):
        before = (q + 3) % 4
        after = (q + 1) % 4
        got(gath.at[a, g, group(before)], ag_s.at[a, g, 3], ag_r.at[a, g, 3])
        half = gath.at[a, g, pl.ds(before * 4, 2)]
        put(half, half, ag_s.at[a, g, 5], ag_r.at[a, g, 5], dev(p, after))
        got(gath.at[a, g, group(after)], ag_s.at[a, g, 4], ag_r.at[a, g, 4])
        half = gath.at[a, g, pl.ds(after * 4 + 2, 2)]
        put(half, half, ag_s.at[a, g, 6], ag_r.at[a, g, 6], dev(p, before))

    def gather_end(a, g):
        far = (q + 2) % 4
        got(gath.at[a, g, pl.ds(far * 4, 2)], ag_s.at[a, g, 5], ag_r.at[a, g, 5])
        got(gath.at[a, g, pl.ds(far * 4 + 2, 2)], ag_s.at[a, g, 6], ag_r.at[a, g, 6])

    def features(slot):
        return ((slot % 4) * 4 + slot // 4) * (1 - c) + slot * c

    def order_vectors():
        for k in range(16):
            at = part(features(k))
            gains[:, k * 256 : (k + 1) * 256] = gain[:, at]
            routes[:, k * 256 : (k + 1) * 256] = router[:, at].astype(F32)

    def project(tick, g, shifts, first):
        sums = jnp.zeros((H, 384), F32) if first else accp[g]
        square = jnp.zeros((H, 128), F32) if first else ssb[g]
        logit = jnp.zeros((H, 128), F32) if first else lgb[g]
        for shift in shifts:
            qq = (q + shift) % 4
            for pp in range(4):
                slot = qq * 4 + pp
                wide = gath[2 * tick, g, slot].astype(F32)
                scaled = (wide * gains[:, part(slot)]).astype(BF16)
                two = wide * wide
                square += two[:, :128] + two[:, 128:]
                two = scaled.astype(F32) * routes[:, part(slot)]
                logit += two[:, :128] + two[:, 128:]
                sums += jnp.dot(scaled, wall[part(slot), :], preferred_element_type=F32)
        return sums, square, logit

    def near(tick, g):
        accp[g], ssb[g], lgb[g] = project(tick, g, (0, 3, 1), True)

    def rope(value, cosine, sine):
        return value * cosine + pltpu.roll(value, 64, 1) * sine

    def rest(tick, g):
        gather_end(2 * tick, g)
        sums, square, logit = project(tick, g, (2,), False)
        rstd = lax.rsqrt(jnp.sum(square, axis=1, keepdims=True) / D + 1e-05)
        kv = (sums[:, 256:] * rstd).astype(BF16)
        kvb[tick, par, rows(g), :] = kv
        mine = kvb.at[tick, par, rows(g), :]
        put(mine, mine, kv_s.at[tick, g, 0], kv_r.at[tick, g, 0], (z, twin * 2 + c))
        put(mine, mine, kv_s.at[tick, g, 1], kv_r.at[tick, g, 1], (z, twin * 2 + 1 - c))
        put(mine, mine, kv_s.at[tick, g, 2], kv_r.at[tick, g, 2], partner)
        cosine = cosb[tick, rows(g), :]
        sine = sinb[tick, rows(g), :]
        query = sums * rstd
        qs[g, :H, :] = rope(query[:, :128], cosine, sine).astype(BF16)
        qs[g, H:, :] = rope(query[:, 128:256], cosine, sine).astype(BF16)
        logit = jnp.sum(logit, axis=1, keepdims=True) * rstd
        slot = lax.broadcasted_iota(jnp.int32, (H, 1), 0) + (g * R + c * H)
        alive = jnp.where(slot < live[:, tick : tick + 1], 1.0, 0.0)
        mixb[g] = jnp.broadcast_to(jax.nn.sigmoid(logit) * alive, (H, 128))

    def attend(tick, g):
        got(kvb.at[tick, 1 - par, rows(g), :], kv_s.at[tick, g, 0], kv_r.at[tick, g, 0])
        got(kvb.at[tick, 1 - par, other_rows(g), :], kv_s.at[tick, g, 1], kv_r.at[tick, g, 1])
        got(kvb.at[tick, par, other_rows(g), :], kv_s.at[tick, g, 2], kv_r.at[tick, g, 2])
        span = slice(g * R, (g + 1) * R)
        low = kvb[tick, 0, span, :].astype(F32)
        high = kvb[tick, 1, span, :].astype(F32)
        left = lax.broadcasted_iota(jnp.int32, (R, 128), 1) < 64
        key = jnp.where(left, low, pltpu.roll(high, 64, 1))
        kc[span, :] = rope(key, cosb[tick, span, :], sinb[tick, span, :]).astype(BF16)
        vc[span, :] = jnp.where(left, pltpu.roll(low, 64, 1), high).astype(BF16)
        upto = (g + 1) * R
        scores = lax.dot_general(
            qs[g], kc[:upto, :], (((1,), (1,)), ((), ())), preferred_element_type=F32
        ) * (1.0 / math.sqrt(HD))
        row = lax.broadcasted_iota(jnp.int32, (2 * H, upto), 0)
        row = jnp.where(row < H, row, row - H) + (g * R + c * H)
        col = lax.broadcasted_iota(jnp.int32, (2 * H, upto), 1)
        scores = jnp.where((col <= row) & (col < live[:, tick : tick + 1]), scores, -jnp.inf)
        top = jnp.max(scores, axis=1, keepdims=True)
        weights = jnp.exp(scores - top)
        probs = (weights / jnp.sum(weights, axis=1, keepdims=True)).astype(BF16)
        result = jnp.dot(probs, vc[:upto, :], preferred_element_type=F32).astype(BF16)
        if tick == 0:
            gath[1, g, own, :, 0:128] = result[:H]
            gath[1, g, own, :, 128:256] = result[H:]
            gather_own(1, g)
        else:
            att[g, p, :, 0:128] = result[:H]
            att[g, p, :, 128:256] = result[H:]
            mine = att.at[g, p]
            for k, d in enumerate((1, 3, 2)):
                put(mine, mine, at_s.at[g, k], at_r.at[g, k], dev((p + d) % 4, q))

    def out_part(g, shifts, first):
        total = jnp.zeros((H, 256), F32) if first else accd[g]
        for shift in shifts:
            qq = (q + shift) % 4
            for pp in range(4):
                slot = qq * 4 + pp
                total += jnp.dot(gath[1, g, slot], woa[part(slot), :], preferred_element_type=F32)
        return total

    def near_out(tick, g):
        accd[g] = out_part(g, (0, 3, 1), True)

    def mix_out(tick, g):
        for k, d in enumerate((1, 3, 2)):
            got(att.at[g, (p + 4 - d) % 4], at_s.at[g, k], at_r.at[g, k])
        for d in (2, 1, 3, 0):
            qq = (q + d) % 4
            total = jnp.zeros((H, 256), F32)
            for pp in range(4):
                total += jnp.dot(att[g, pp], wod[qq, pp], preferred_element_type=F32)
            if d == 0:
                accd[g] = total
            else:
                rss[g, d - 1] = total.astype(BF16)
                put(
                    rss.at[g, d - 1], rsr.at[g, d - 1], rs_s.at[g, d - 1], rs_r.at[g, d - 1],
                    dev(p, qq),
                )

    def rest_out(tick, g):
        gather_end(2 * tick + 1, g)
        delta = out_part(g, (2,), False)
        update(tick, g, delta)

    def finish(tick, g):
        delta = accd[g]
        for d in (1, 3, 2):
            got(rsr.at[g, d - 1], rs_s.at[g, d - 1], rs_r.at[g, d - 1])
            delta += rsr[g, d - 1].astype(F32)
        update(tick, g, delta)

    def update(tick, g, delta):
        mixing = jnp.concatenate([mixb[g], mixb[g]], axis=1)
        new = (gath[2 * tick, g, own].astype(F32) + mixing * delta).astype(BF16)
        if tick == 0:
            ub[g] = new
            put(ub.at[g], u0.at[rows(g), :], uz_s.at[g, 0], uz_r.at[g, 0], (znext, t))
            put(ub.at[g], u0.at[rows(g), :], uz_s.at[g, 1], uz_r.at[g, 1], (znext, other))
        else:
            low, high = new[:, :128].astype(F32), new[:, 128:].astype(F32)
            u1s[g] = (high * (1 - cf) + low * cf).astype(BF16)
            put(u1s.at[g], u1.at[rows(g), :], e_s.at[g], e_r.at[g], partner)
            u1[rows(g), :] = (low * (1 - cf) + high * cf).astype(BF16)

    def tables(tick):
        for g in range(CAP // 128):
            span = slice(g * 128, (g + 1) * 128)
            angle = lsp[tick, span, :] * freq[...]
            sign = jnp.where(lax.broadcasted_iota(jnp.int32, (128, 128), 1) < 64, -1.0, 1.0)
            cosb[tick, span, :] = jnp.cos(angle)
            sinb[tick, span, :] = jnp.sin(angle) * sign

    def place_kv():
        cp_wk.wait()
        cp_wv.wait()
        row = lax.broadcasted_iota(jnp.int32, (64, 128), 0)
        col = lax.broadcasted_iota(jnp.int32, (64, 128), 1)
        row = jnp.where(row < 32, row, row + 32) + 32 * c
        hot = jnp.where(col == row, 1.0, 0.0).astype(BF16)

        def some(k, _):
            at = pl.ds(pl.multiple_of(k * 512, 512), 512)
            both = jnp.concatenate([wkl[:, at], wvl[:, at]], axis=0)
            w2o[at, :] = lax.dot_general(both, hot, (((0,), (0,)), ((), ())), preferred_element_type=F32).astype(BF16)
            return 0

        lax.fori_loop(0, D // 512, some, 0)

    def ready_weights():
        pltpu.make_async_copy(wq, wall.at[:, mycols], loc.at[3]).wait()
        got(wall.at[:, theircols], wx_s.at[0], wx_r.at[0])
        got(w2p, wx_s.at[1], wx_r.at[1])

        def some(k, _):
            wall[part(k), 256:] = w2o[part(features(k)), :] + w2p[part(k), :]
            return 0

        lax.fori_loop(0, 16, some, 0)

    def ready_wo():
        pltpu.make_async_copy(wo, woa.at[:, mycols], loc.at[4]).wait()
        got(woa.at[:, theircols], wx_s.at[2], wx_r.at[2])

    def ready_ring():
        pltpu.make_async_copy(wod.at[q, :, :, mycols], wod.at[q, :, :, mycols], loc.at[6]).wait()
        got(wod.at[q, :, :, theircols], wo_s.at[0, 1], wo_r.at[0, 1])
        for d in (1, 3, 2):
            from_q = (q + 4 - d) % 4
            got(wod.at[from_q, :, :, mycols], wo_s.at[d, 0], wo_r.at[d, 0])
            got(wod.at[from_q, :, :, theircols], wo_s.at[d, 1], wo_r.at[d, 1])

    def token_map():
        row = chosen[1:2, :].astype(F32)

        def some(k, _):
            token = (lax.broadcasted_iota(jnp.int32, (256, CAP), 0) + k * 256).astype(F32)
            hot = jnp.where(token == row, 1.0, 0.0).astype(BF16)
            mt[part(k), :] = hot
            facc[part(k), :] = 1.0 - jnp.dot(hot, jnp.ones((CAP, 128), BF16), preferred_element_type=F32)
            return 0

        lax.fori_loop(0, TOKENS // 256, some, 0)

    def base_rows():
        cp_inc.wait()
        got(bulk, wx_s.at[4], wx_r.at[4])
        got(lprev, wx_s.at[3], wx_r.at[3])

        def some(k, _):
            mixed = bulk[part(k), :].astype(F32) * zf + inc[part(k), :].astype(F32) * (1 - zf)
            strm[part(k), :] = mixed.astype(BF16)
            return 0

        lax.fori_loop(0, TOKENS // 256, some, 0)

    def base_take(g):
        mine, others = mine_of(take_rows(1, g, lambda k: strm[k * 256 : (k + 1) * 256, :]))
        bp[g, :, mycols] = mine
        pst[1, g] = others
        put(pst.at[1, g], bp.at[g, :, mycols], pk_s.at[1, g], pk_r.at[1, g], partner)

    def previous():
        return lprev[0:1, :].astype(F32) * zf - (1 - zf)

    def base_kept(g):
        got(bp.at[g, :, theircols], pk_s.at[1, g], pk_r.at[1, g])
        pos = lsp[1, rows(g), :]
        pos = jnp.concatenate([pos] * (CAP // 128), axis=1)
        hot = jnp.where(pos == previous(), 1.0, 0.0)
        same[g * H : (g + 1) * H, :] = hot.astype(BF16)
        accm[g * H : (g + 1) * H, :] = bp[g].astype(F32) * (1.0 - jnp.sum(hot, axis=1, keepdims=True))

    def base_moved(g):
        got(u0.at[rows(g), :], uz_s.at[g, 0], uz_r.at[g, 0])
        got(u0.at[other_rows(g), :], uz_s.at[g, 1], uz_r.at[g, 1])
        span = slice(g * R, (g + 1) * R)
        total = accm[...] + jnp.dot(same[:, span], u0[span, :], preferred_element_type=F32)
        if g < N - 1:
            accm[...] = total
        else:
            for k in range(N):
                gath[2, k, own] = total[k * H : (k + 1) * H].astype(BF16)
                gather_own(2, k)

    def unlisted(first, last):
        both = jnp.concatenate([u0[:, mycols], jnp.ones((CAP, 128), BF16)], axis=1)
        row = previous()

        def some(k, _):
            token = (lax.broadcasted_iota(jnp.int32, (256, CAP), 0) + k * 256).astype(F32)
            hot = jnp.where(token == row, 1.0, 0.0).astype(BF16)
            moved = jnp.dot(hot, both, preferred_element_type=F32)
            state = strm[part(k), :].astype(F32) * (1.0 - moved[:, 128:]) + moved[:, :128]
            facc[part(k), :] = state * facc[part(k), :]
            return 0

        lax.fori_loop(first, last, some, 0)

    def write(g):
        got(u1.at[other_rows(g), :], e_s.at[g], e_r.at[g])
        span = slice(g * R, (g + 1) * R)

        def some(k, _):
            total = facc[part(k), :] + jnp.dot(mt[part(k), span], u1[span, :], preferred_element_type=F32)
            if g < N - 1:
                facc[part(k), :] = total
            else:
                out[part(k), :] = total.astype(BF16)
            return 0

        lax.fori_loop(0, TOKENS // 256, some, 0)

    def pick(g):
        mine, others = mine_of(take_rows(0, g, lambda k: strm[k * 256 : (k + 1) * 256, :]))
        gath[0, g, own, :, mycols] = mine
        pst[0, g] = others

    def swap(g):
        put(pst.at[0, g], gath.at[0, g, p * 4 + q, :, mycols], pk_s.at[0, g], pk_r.at[0, g], partner)

    def swapped(g):
        got(gath.at[0, g, own, :, theircols], pk_s.at[0, g], pk_r.at[0, g])

    spread(0)
    cp_strm.wait()
    pick(0)
    pl.semaphore_wait(barrier, len(peers))
    swap(0)
    pick(1)
    swap(1)
    swapped(0)
    gather_own(0, 0)
    swapped(1)
    gather_own(0, 1)
    put_out(wq, wall, mycols, 0)
    put(chosen, lprev, wx_s.at[3], wx_r.at[3], (znext, t))
    put(stream, bulk, wx_s.at[4], wx_r.at[4], (znext, t))
    order_vectors()
    gather_group(0, 0)
    gather_group(0, 1)
    place_kv()
    put_out(w2o, w2p, slice(None), 1)
    gather_far(0, 0)
    lay_out(wo, woa, loc.at[4])
    put_out(wo, woa, mycols, 2)
    tables(0)
    gather_far(0, 1)
    ready_weights()
    near(0, 0)
    rest(0, 0)
    near(0, 1)
    rest(0, 1)
    attend(0, 0)
    attend(0, 1)
    spread(1)
    base_rows()
    gather_group(1, 0)
    gather_group(1, 1)
    base_take(0)
    base_take(1)
    tables(1)
    gather_far(1, 0)
    token_map()
    gather_far(1, 1)
    ready_wo()
    out_weights(1)
    near_out(0, 0)
    base_kept(0)
    rest_out(0, 0)
    base_kept(1)
    near_out(0, 1)
    base_moved(0)
    rest_out(0, 1)
    out_weights(3)
    out_weights(0)
    base_moved(1)
    gather_group(2, 0)
    gather_group(2, 1)
    gather_far(2, 0)
    unlisted(0, 4)
    gather_far(2, 1)
    near(1, 0)
    rest(1, 0)
    near(1, 1)
    rest(1, 1)
    out_weights(2)
    attend(1, 0)
    attend(1, 1)
    unlisted(4, 8)
    ready_ring()
    mix_out(1, 0)
    mix_out(1, 1)
    finish(1, 0)
    write(0)
    finish(1, 1)
    write(1)
    for cp in sends:
        cp.wait_send()


def body(stream, incoming, chosen, live, norm_gain, router, wq, wk, wv, wo):
    half = HD // 2
    freq = np.exp(-math.log(500000.0) * 2.0 * np.arange(half) / HD)
    freq = jnp.asarray(np.concatenate([freq, freq])[None, :], F32)
    vmem = pl.BlockSpec(memory_space=pltpu.VMEM)
    hbm = pl.BlockSpec(memory_space=pl.ANY)
    dma = pltpu.SemaphoreType.DMA
    scratch = [
        pltpu.VMEM((TOKENS, 128), BF16),
        pltpu.VMEM((TOKENS, 128), BF16),
        pltpu.VMEM((TOKENS, 128), BF16),
        pltpu.VMEM((D, 384), BF16),
        pltpu.VMEM((D, 256), BF16),
        pltpu.VMEM((4, 4, 256, 256), BF16),
        pltpu.VMEM((32, D), BF16),
        pltpu.VMEM((32, D), BF16),
        pltpu.VMEM((D, 128), BF16),
        pltpu.VMEM((D, 128), BF16),
        pltpu.VMEM((1, D), F32),
        pltpu.VMEM((1, D), F32),
        pltpu.VMEM((N * H, CAP), BF16),
        pltpu.VMEM((2, CAP), jnp.int32),
        pltpu.VMEM((2, CAP, 128), F32),
        pltpu.VMEM((2, CAP, 128), F32),
        pltpu.VMEM((2, CAP, 128), F32),
        pltpu.VMEM((3, N, 16, H, 256), BF16),
        pltpu.VMEM((N, 4, H, 256), BF16),
        pltpu.VMEM((N, 3, H, 256), BF16),
        pltpu.VMEM((N, 3, H, 256), BF16),
        pltpu.VMEM((2, N, H, 128), BF16),
        pltpu.VMEM((N, H, 256), BF16),
        pltpu.VMEM((2, 2, CAP, 128), BF16),
        pltpu.VMEM((CAP, 128), BF16),
        pltpu.VMEM((CAP, 128), BF16),
        pltpu.VMEM((N, 2 * H, 128), BF16),
        pltpu.VMEM((N, H, 384), F32),
        pltpu.VMEM((N, H, 128), F32),
        pltpu.VMEM((N, H, 128), F32),
        pltpu.VMEM((N, H, 128), F32),
        pltpu.VMEM((N, H, 256), F32),
        pltpu.VMEM((N, H, 256), BF16),
        pltpu.VMEM((N * H, 256), F32),
        pltpu.VMEM((CAP, 256), BF16),
        pltpu.VMEM((N, H, 128), BF16),
        pltpu.VMEM((CAP, 128), BF16),
        pltpu.VMEM((TOKENS, CAP), BF16),
        pltpu.VMEM((TOKENS, 128), F32),
        dma((7,)),
        dma((3, N, 7)),
        dma((3, N, 7)),
        dma((N, 3)),
        dma((N, 3)),
        dma((N, 3)),
        dma((N, 3)),
        dma((4, 2)),
        dma((4, 2)),
        dma((2, N)),
        dma((2, N)),
        dma((2, N, 3)),
        dma((2, N, 3)),
        dma((N, 2)),
        dma((N, 2)),
        dma((5,)),
        dma((5,)),
        dma((N,)),
        dma((N,)),
    ]
    result = pl.pallas_call(
        kernel,
        out_shape=jax.ShapeDtypeStruct((TOKENS, 128), BF16),
        in_specs=[hbm, hbm, vmem, vmem, vmem, vmem, vmem, hbm, hbm, hbm, hbm],
        out_specs=vmem,
        scratch_shapes=scratch,
        compiler_params=pltpu.CompilerParams(
            collective_id=0, has_side_effects=True, vmem_limit_bytes=62 * 2**20
        ),
        name="relay",
    )(stream[0], incoming[0], chosen[0], live, norm_gain, router, freq, wq[0], jnp.swapaxes(wk[0], 0, 1), jnp.swapaxes(wv[0], 0, 1), wo[0])
    return result[None]


def solution(mesh):
    in_specs = (
        P("pipe", None, "tp"),
        P(None, None, "tp"),
        P("pipe", None, None),
        P("pipe", None),
        P("pipe", None),
        P("pipe", None),
        P("pipe", None, "tp"),
        P("pipe", None, "tp"),
        P("pipe", None, "tp"),
        P("pipe", None, "tp"),
    )
    out_specs = P("pipe", None, "tp")
    return jax.shard_map(body, mesh=mesh, in_specs=in_specs, out_specs=out_specs, check_vma=False)
```

```python
import functools
import math

import jax
import jax.numpy as jnp
import numpy as np
from jax import lax
from jax.experimental import pallas as pl
from jax.experimental.pallas import tpu as pltpu
from jax.sharding import PartitionSpec as P

MESH = pl.DeviceIdType.MESH
F32 = jnp.float32
BF16 = jnp.bfloat16

D = 4096
TOKENS = 2048
CAP = 512
HD = 128
N = 2
R = CAP // N
H = R // 2


def kernel(
    stream, incoming, chosen, live, gain, router, freq, wq, wk, wv, wo, out,
    strm, inc, bulk, wall, woa, wod, wkl, wvl, w2o, w2p, gains, routes, same, lprev, lsp, cosb, sinb, gath, att, rss, rsr, pst, bp, kvb, kc, vc,
    qs, accp, ssb, lgb, mixb, accd, ub, accm, u0, u1s, u1, mt, facc,
    loc, ag_s, ag_r, at_s, at_r, rs_s, rs_r, wo_s, wo_r, pk_s, pk_r, kv_s, kv_r, uz_s, uz_r, wx_s, wx_r, e_s, e_r,
):
    z = lax.axis_index("pipe")
    t = lax.axis_index("tp")
    nz = lax.axis_size("pipe")
    c = t % 2
    chip = t // 2
    y = chip % 4
    x = chip // 4
    p = x * (1 - c) + y * c
    q = y * (1 - c) + x * c
    own = q * 4 + p
    partner = (z, chip * 2 + 1 - c)
    par = y % 2
    twin = x * 4 + y + 1 - 2 * par

    def dev(pp, qq):
        xx = pp * (1 - c) + qq * c
        yy = qq * (1 - c) + pp * c
        return (z, (xx * 4 + yy) * 2 + c)

    def cross(pp, qq):
        xx = pp * (1 - c) + qq * c
        yy = qq * (1 - c) + pp * c
        return (z, (xx * 4 + yy) * 2 + 1 - c)

    znext = (z + 1) % nz
    zprev = (z + nz - 1) % nz
    other = chip * 2 + 1 - c

    barrier = pltpu.get_barrier_semaphore()
    peers = [dev((p + d) % 4, q) for d in (1, 2, 3)] + [dev(p, (q + d) % 4) for d in (1, 2, 3)]
    peers += [cross((p + d) % 4, q) for d in (1, 2, 3)] + [cross(p, (q + d) % 4) for d in (1, 2, 3)] + [partner]
    peers += [(znext, t), (znext, other), (zprev, t), (zprev, other)]
    for peer in peers:
        pl.semaphore_signal(barrier, inc=1, device_id=peer, device_id_type=MESH)

    sends = []

    def put(src, dst, s_sem, r_sem, device):
        cp = pltpu.make_async_remote_copy(
            src_ref=src, dst_ref=dst, send_sem=s_sem, recv_sem=r_sem, device_id=device, device_id_type=MESH
        )
        cp.start()
        sends.append(cp)

    def got(dst, s_sem, r_sem):
        pltpu.make_async_remote_copy(
            src_ref=dst, dst_ref=dst, send_sem=s_sem, recv_sem=r_sem, device_id=partner, device_id_type=MESH
        ).wait_recv()

    mycols = pl.ds(pl.multiple_of(c * 128, 128), 128)

    def local(k, src, dst):
        cp = pltpu.make_async_copy(src, dst, loc.at[k])
        cp.start()
        return cp

    cp_strm = local(0, stream, strm)
    cp_wk = local(1, wk, wkl)
    cp_wv = local(2, wv, wvl)
    cp_inc = local(5, incoming, inc)

    def slot_of(k, cc):
        return ((k % 4) * 4 + k // 4) * (1 - cc) + k * cc

    def part(k):
        return pl.ds(pl.multiple_of(k * 256, 256), 256)

    def lay_out(source, target, sem):
        def some(k, _):
            pltpu.make_async_copy(source.at[part(k), :], target.at[part(slot_of(k, c)), mycols], sem).start()
            return 0

        lax.fori_loop(0, 16, some, 0)

    lay_out(wq, wall, loc.at[3])

    def put_out(source, target, columns, k):
        def some(i, _):
            pltpu.make_async_remote_copy(
                src_ref=source.at[part(i), :], dst_ref=target.at[part(slot_of(i, 1 - c)), columns],
                send_sem=wx_s.at[k], recv_sem=wx_r.at[k], device_id=partner, device_id_type=MESH,
            ).start()
            return 0

        lax.fori_loop(0, 16, some, 0)
        whole = target.at[:, columns]
        sends.append(
            pltpu.make_async_remote_copy(
                src_ref=whole, dst_ref=whole, send_sem=wx_s.at[k], recv_sem=wx_r.at[k],
                device_id=partner, device_id_type=MESH,
            )
        )

    def chip_of(pp, qq, cc):
        return (pp * 4 + qq) * (1 - cc) + (qq * 4 + pp) * cc

    def out_weights(d):
        qq = (q + d) % 4
        pp = (p + d) % 4
        for k in range(4):
            if d == 0:
                pltpu.make_async_copy(wo.at[part(chip_of(k, qq, c)), :], wod.at[q, k, :, mycols], loc.at[6]).start()
            else:
                pltpu.make_async_remote_copy(
                    src_ref=wo.at[part(chip_of(k, qq, c)), :], dst_ref=wod.at[q, k, :, mycols],
                    send_sem=wo_s.at[d, 0], recv_sem=wo_r.at[d, 0], device_id=dev(p, qq), device_id_type=MESH,
                ).start()
            pltpu.make_async_remote_copy(
                src_ref=wo.at[part(chip_of(k, pp, 1 - c)), :], dst_ref=wod.at[p, k, :, mycols],
                send_sem=wo_s.at[d, 1], recv_sem=wo_r.at[d, 1], device_id=cross(pp, q), device_id_type=MESH,
            ).start()
        for way in range(2):
            if d or way:
                whole = wod.at[0, :, :, mycols]
                sends.append(
                    pltpu.make_async_remote_copy(
                        src_ref=whole, dst_ref=whole, send_sem=wo_s.at[d, way], recv_sem=wo_r.at[d, way],
                        device_id=partner, device_id_type=MESH,
                    )
                )

    theircols = pl.ds(pl.multiple_of((1 - c) * 128, 128), 128)
    zf = jnp.minimum(z, 1).astype(F32)
    cf = c.astype(F32)

    def rows(g):
        return pl.ds(pl.multiple_of(g * R + c * H, H), H)

    def other_rows(g):
        return pl.ds(pl.multiple_of(g * R + (1 - c) * H, H), H)

    def spread(tick):
        row = chosen[tick : tick + 1, :].astype(F32)
        for k in range(CAP // 128):
            lsp[tick, k * 128 : (k + 1) * 128, :] = jnp.transpose(
                jnp.broadcast_to(row[:, k * 128 : (k + 1) * 128], (128, 128))
            )

    def take_rows(tick, g, source):
        lane = lax.broadcasted_iota(jnp.int32, (R, 256), 1).astype(F32)
        pos = lsp[tick, g * R : (g + 1) * R, :]
        pos = jnp.concatenate([pos, pos], axis=1)
        total = jnp.zeros((R, 128), F32)
        for k in range(TOKENS // 256):
            hot = jnp.where(pos == lane + float(k * 256), 1.0, 0.0).astype(BF16)
            total += jnp.dot(hot, source(k), preferred_element_type=F32)
        return total

    def mine_of(value):
        low, high = value[:H], value[H:]
        return (low * (1 - cf) + high * cf).astype(BF16), (high * (1 - cf) + low * cf).astype(BF16)

    def pass_on(a, g, block):
        for k, d in ((3, 1), (4, 3)):
            pltpu.make_async_remote_copy(
                src_ref=gath.at[a, g, block], dst_ref=gath.at[a, g, block], send_sem=ag_s.at[a, g, k],
                recv_sem=ag_r.at[a, g, k], device_id=dev(p, (q + d) % 4), device_id_type=MESH,
            ).start()

    def gather_own(a, g):
        for k, d in enumerate((1, 3, 2)):
            put(gath.at[a, g, own], gath.at[a, g, own], ag_s.at[a, g, k], ag_r.at[a, g, k], dev((p + d) % 4, q))
        pass_on(a, g, own)

    def group(qq):
        return pl.ds(qq * 4, 4)

    def gather_group(a, g):
        for k, d in enumerate((1, 3, 2)):
            block = q * 4 + (p + 4 - d) % 4
            got(gath.at[a, g, block], ag_s.at[a, g, k], ag_r.at[a, g, k])
            pass_on(a, g, block)
        for k in (3, 4):
            mine = gath.at[a, g, group(q)]
            sends.append(
                pltpu.make_async_remote_copy(
                    src_ref=mine, dst_ref=mine, send_sem=ag_s.at[a, g, k], recv_sem=ag_r.at[a, g, k],
                    device_id=partner, device_id_type=MESH,
                )
            )

    def gather_far(a, g):
        before = (q + 3) % 4
        after = (q + 1) % 4
        got(gath.at[a, g, group(before)], ag_s.at[a, g, 3], ag_r.at[a, g, 3])
        half = gath.at[a, g, pl.ds(before * 4, 2)]
        put(half, half, ag_s.at[a, g, 5], ag_r.at[a, g, 5], dev(p, after))
        got(gath.at[a, g, group(after)], ag_s.at[a, g, 4], ag_r.at[a, g, 4])
        half = gath.at[a, g, pl.ds(after * 4 + 2, 2)]
        put(half, half, ag_s.at[a, g, 6], ag_r.at[a, g, 6], dev(p, before))

    def gather_end(a, g):
        far = (q + 2) % 4
        got(gath.at[a, g, pl.ds(far * 4, 2)], ag_s.at[a, g, 5], ag_r.at[a, g, 5])
        got(gath.at[a, g, pl.ds(far * 4 + 2, 2)], ag_s.at[a, g, 6], ag_r.at[a, g, 6])

    def features(slot):
        return ((slot % 4) * 4 + slot // 4) * (1 - c) + slot * c

    def order_vectors():
        for k in range(16):
            at = part(features(k))
            gains[:, k * 256 : (k + 1) * 256] = gain[:, at]
            routes[:, k * 256 : (k + 1) * 256] = router[:, at].astype(F32)

    def project(tick, g, shifts, first):
        sums = jnp.zeros((H, 384), F32) if first else accp[g]
        square = jnp.zeros((H, 128), F32) if first else ssb[g]
        logit = jnp.zeros((H, 128), F32) if first else lgb[g]
        for shift in shifts:
            qq = (q + shift) % 4
            for pp in range(4):
                slot = qq * 4 + pp
                wide = gath[2 * tick, g, slot].astype(F32)
                scaled = (wide * gains[:, part(slot)]).astype(BF16)
                two = wide * wide
                square += two[:, :128] + two[:, 128:]
                two = scaled.astype(F32) * routes[:, part(slot)]
                logit += two[:, :128] + two[:, 128:]
                sums += jnp.dot(scaled, wall[part(slot), :], preferred_element_type=F32)
        return sums, square, logit

    def near(tick, g):
        accp[g], ssb[g], lgb[g] = project(tick, g, (0, 3, 1), True)

    def rope(value, cosine, sine):
        return value * cosine + pltpu.roll(value, 64, 1) * sine

    def rest(tick, g):
        gather_end(2 * tick, g)
        sums, square, logit = project(tick, g, (2,), False)
        rstd = lax.rsqrt(jnp.sum(square, axis=1, keepdims=True) / D + 1e-05)
        kv = (sums[:, 256:] * rstd).astype(BF16)
        kvb[tick, par, rows(g), :] = kv
        mine = kvb.at[tick, par, rows(g), :]
        put(mine, mine, kv_s.at[tick, g, 0], kv_r.at[tick, g, 0], (z, twin * 2 + c))
        put(mine, mine, kv_s.at[tick, g, 1], kv_r.at[tick, g, 1], (z, twin * 2 + 1 - c))
        put(mine, mine, kv_s.at[tick, g, 2], kv_r.at[tick, g, 2], partner)
        cosine = cosb[tick, rows(g), :]
        sine = sinb[tick, rows(g), :]
        query = sums * rstd
        qs[g, :H, :] = rope(query[:, :128], cosine, sine).astype(BF16)
        qs[g, H:, :] = rope(query[:, 128:256], cosine, sine).astype(BF16)
        logit = jnp.sum(logit, axis=1, keepdims=True) * rstd
        slot = lax.broadcasted_iota(jnp.int32, (H, 1), 0) + (g * R + c * H)
        alive = jnp.where(slot < live[:, tick : tick + 1], 1.0, 0.0)
        mixb[g] = jnp.broadcast_to(jax.nn.sigmoid(logit) * alive, (H, 128))

    def attend(tick, g):
        got(kvb.at[tick, 1 - par, rows(g), :], kv_s.at[tick, g, 0], kv_r.at[tick, g, 0])
        got(kvb.at[tick, 1 - par, other_rows(g), :], kv_s.at[tick, g, 1], kv_r.at[tick, g, 1])
        got(kvb.at[tick, par, other_rows(g), :], kv_s.at[tick, g, 2], kv_r.at[tick, g, 2])
        span = slice(g * R, (g + 1) * R)
        low = kvb[tick, 0, span, :].astype(F32)
        high = kvb[tick, 1, span, :].astype(F32)
        left = lax.broadcasted_iota(jnp.int32, (R, 128), 1) < 64
        key = jnp.where(left, low, pltpu.roll(high, 64, 1))
        kc[span, :] = rope(key, cosb[tick, span, :], sinb[tick, span, :]).astype(BF16)
        vc[span, :] = jnp.where(left, pltpu.roll(low, 64, 1), high).astype(BF16)
        upto = (g + 1) * R
        scores = lax.dot_general(
            qs[g], kc[:upto, :], (((1,), (1,)), ((), ())), preferred_element_type=F32
        ) * (1.0 / math.sqrt(HD))
        row = lax.broadcasted_iota(jnp.int32, (2 * H, upto), 0)
        row = jnp.where(row < H, row, row - H) + (g * R + c * H)
        col = lax.broadcasted_iota(jnp.int32, (2 * H, upto), 1)
        scores = jnp.where((col <= row) & (col < live[:, tick : tick + 1]), scores, -jnp.inf)
        top = jnp.max(scores, axis=1, keepdims=True)
        weights = jnp.exp(scores - top)
        probs = (weights / jnp.sum(weights, axis=1, keepdims=True)).astype(BF16)
        result = jnp.dot(probs, vc[:upto, :], preferred_element_type=F32).astype(BF16)
        if tick == 0:
            gath[1, g, own, :, 0:128] = result[:H]
            gath[1, g, own, :, 128:256] = result[H:]
            gather_own(1, g)
        else:
            att[g, p, :, 0:128] = result[:H]
            att[g, p, :, 128:256] = result[H:]
            mine = att.at[g, p]
            for k, d in enumerate((1, 3, 2)):
                put(mine, mine, at_s.at[g, k], at_r.at[g, k], dev((p + d) % 4, q))

    def out_part(g, shifts, first):
        total = jnp.zeros((H, 256), F32) if first else accd[g]
        for shift in shifts:
            qq = (q + shift) % 4
            for pp in range(4):
                slot = qq * 4 + pp
                total += jnp.dot(gath[1, g, slot], woa[part(slot), :], preferred_element_type=F32)
        return total

    def near_out(tick, g):
        accd[g] = out_part(g, (0, 3, 1), True)

    def mix_out(tick, g):
        for k, d in enumerate((1, 3, 2)):
            got(att.at[g, (p + 4 - d) % 4], at_s.at[g, k], at_r.at[g, k])
        for d in (2, 1, 3, 0):
            qq = (q + d) % 4
            total = jnp.zeros((H, 256), F32)
            for pp in range(4):
                total += jnp.dot(att[g, pp], wod[qq, pp], preferred_element_type=F32)
            if d == 0:
                accd[g] = total
            else:
                rss[g, d - 1] = total.astype(BF16)
                put(
                    rss.at[g, d - 1], rsr.at[g, d - 1], rs_s.at[g, d - 1], rs_r.at[g, d - 1],
                    dev(p, qq),
                )

    def rest_out(tick, g):
        gather_end(2 * tick + 1, g)
        delta = out_part(g, (2,), False)
        update(tick, g, delta)

    def finish(tick, g):
        delta = accd[g]
        for d in (1, 3, 2):
            got(rsr.at[g, d - 1], rs_s.at[g, d - 1], rs_r.at[g, d - 1])
            delta += rsr[g, d - 1].astype(F32)
        update(tick, g, delta)

    def update(tick, g, delta):
        mixing = jnp.concatenate([mixb[g], mixb[g]], axis=1)
        new = (gath[2 * tick, g, own].astype(F32) + mixing * delta).astype(BF16)
        if tick == 0:
            ub[g] = new
            put(ub.at[g], u0.at[rows(g), :], uz_s.at[g, 0], uz_r.at[g, 0], (znext, t))
            put(ub.at[g], u0.at[rows(g), :], uz_s.at[g, 1], uz_r.at[g, 1], (znext, other))
        else:
            low, high = new[:, :128].astype(F32), new[:, 128:].astype(F32)
            u1s[g] = (high * (1 - cf) + low * cf).astype(BF16)
            put(u1s.at[g], u1.at[rows(g), :], e_s.at[g], e_r.at[g], partner)
            u1[rows(g), :] = (low * (1 - cf) + high * cf).astype(BF16)

    def tables(tick):
        for g in range(CAP // 128):
            span = slice(g * 128, (g + 1) * 128)
            angle = lsp[tick, span, :] * freq[...]
            sign = jnp.where(lax.broadcasted_iota(jnp.int32, (128, 128), 1) < 64, -1.0, 1.0)
            cosb[tick, span, :] = jnp.cos(angle)
            sinb[tick, span, :] = jnp.sin(angle) * sign

    def place_kv():
        cp_wk.wait()
        cp_wv.wait()
        row = lax.broadcasted_iota(jnp.int32, (64, 128), 0)
        col = lax.broadcasted_iota(jnp.int32, (64, 128), 1)
        row = jnp.where(row < 32, row, row + 32) + 32 * c
        hot = jnp.where(col == row, 1.0, 0.0).astype(BF16)

        def some(k, _):
            at = pl.ds(pl.multiple_of(k * 512, 512), 512)
            both = jnp.concatenate([wkl[:, at], wvl[:, at]], axis=0)
            w2o[at, :] = lax.dot_general(both, hot, (((0,), (0,)), ((), ())), preferred_element_type=F32).astype(BF16)
            return 0

        lax.fori_loop(0, D // 512, some, 0)

    def ready_weights():
        pltpu.make_async_copy(wq, wall.at[:, mycols], loc.at[3]).wait()
        got(wall.at[:, theircols], wx_s.at[0], wx_r.at[0])
        got(w2p, wx_s.at[1], wx_r.at[1])

        def some(k, _):
            wall[part(k), 256:] = w2o[part(features(k)), :] + w2p[part(k), :]
            return 0

        lax.fori_loop(0, 16, some, 0)

    def ready_wo():
        pltpu.make_async_copy(wo, woa.at[:, mycols], loc.at[4]).wait()
        got(woa.at[:, theircols], wx_s.at[2], wx_r.at[2])

    def ready_ring():
        pltpu.make_async_copy(wod.at[q, :, :, mycols], wod.at[q, :, :, mycols], loc.at[6]).wait()
        got(wod.at[q, :, :, theircols], wo_s.at[0, 1], wo_r.at[0, 1])
        for d in (1, 3, 2):
            from_q = (q + 4 - d) % 4
            got(wod.at[from_q, :, :, mycols], wo_s.at[d, 0], wo_r.at[d, 0])
            got(wod.at[from_q, :, :, theircols], wo_s.at[d, 1], wo_r.at[d, 1])

    def token_map():
        row = chosen[1:2, :].astype(F32)

        def some(k, _):
            token = (lax.broadcasted_iota(jnp.int32, (256, CAP), 0) + k * 256).astype(F32)
            hot = jnp.where(token == row, 1.0, 0.0).astype(BF16)
            mt[part(k), :] = hot
            facc[part(k), :] = 1.0 - jnp.dot(hot, jnp.ones((CAP, 128), BF16), preferred_element_type=F32)
            return 0

        lax.fori_loop(0, TOKENS // 256, some, 0)

    def base_rows():
        cp_inc.wait()
        got(bulk, wx_s.at[4], wx_r.at[4])
        got(lprev, wx_s.at[3], wx_r.at[3])

        def some(k, _):
            mixed = bulk[part(k), :].astype(F32) * zf + inc[part(k), :].astype(F32) * (1 - zf)
            strm[part(k), :] = mixed.astype(BF16)
            return 0

        lax.fori_loop(0, TOKENS // 256, some, 0)

    def base_take(g):
        mine, others = mine_of(take_rows(1, g, lambda k: strm[k * 256 : (k + 1) * 256, :]))
        bp[g, :, mycols] = mine
        pst[1, g] = others
        put(pst.at[1, g], bp.at[g, :, mycols], pk_s.at[1, g], pk_r.at[1, g], partner)

    def previous():
        return lprev[0:1, :].astype(F32) * zf - (1 - zf)

    def base_kept(g):
        got(bp.at[g, :, theircols], pk_s.at[1, g], pk_r.at[1, g])
        pos = lsp[1, rows(g), :]
        pos = jnp.concatenate([pos] * (CAP // 128), axis=1)
        hot = jnp.where(pos == previous(), 1.0, 0.0)
        same[g * H : (g + 1) * H, :] = hot.astype(BF16)
        accm[g * H : (g + 1) * H, :] = bp[g].astype(F32) * (1.0 - jnp.sum(hot, axis=1, keepdims=True))

    def base_moved(g):
        got(u0.at[rows(g), :], uz_s.at[g, 0], uz_r.at[g, 0])
        got(u0.at[other_rows(g), :], uz_s.at[g, 1], uz_r.at[g, 1])
        span = slice(g * R, (g + 1) * R)
        total = accm[...] + jnp.dot(same[:, span], u0[span, :], preferred_element_type=F32)
        if g < N - 1:
            accm[...] = total
        else:
            for k in range(N):
                gath[2, k, own] = total[k * H : (k + 1) * H].astype(BF16)
                gather_own(2, k)

    def unlisted(first, last):
        both = jnp.concatenate([u0[:, mycols], jnp.ones((CAP, 128), BF16)], axis=1)
        row = previous()

        def some(k, _):
            token = (lax.broadcasted_iota(jnp.int32, (256, CAP), 0) + k * 256).astype(F32)
            hot = jnp.where(token == row, 1.0, 0.0).astype(BF16)
            moved = jnp.dot(hot, both, preferred_element_type=F32)
            state = strm[part(k), :].astype(F32) * (1.0 - moved[:, 128:]) + moved[:, :128]
            facc[part(k), :] = state * facc[part(k), :]
            return 0

        lax.fori_loop(first, last, some, 0)

    def write(g):
        got(u1.at[other_rows(g), :], e_s.at[g], e_r.at[g])
        span = slice(g * R, (g + 1) * R)

        def some(k, _):
            total = facc[part(k), :] + jnp.dot(mt[part(k), span], u1[span, :], preferred_element_type=F32)
            if g < N - 1:
                facc[part(k), :] = total
            else:
                out[part(k), :] = total.astype(BF16)
            return 0

        lax.fori_loop(0, TOKENS // 256, some, 0)

    def pick(g):
        mine, others = mine_of(take_rows(0, g, lambda k: strm[k * 256 : (k + 1) * 256, :]))
        gath[0, g, own, :, mycols] = mine
        pst[0, g] = others

    def swap(g):
        put(pst.at[0, g], gath.at[0, g, p * 4 + q, :, mycols], pk_s.at[0, g], pk_r.at[0, g], partner)

    def swapped(g):
        got(gath.at[0, g, own, :, theircols], pk_s.at[0, g], pk_r.at[0, g])

    spread(0)
    cp_strm.wait()
    pick(0)
    pl.semaphore_wait(barrier, len(peers))
    swap(0)
    pick(1)
    swap(1)
    swapped(0)
    gather_own(0, 0)
    swapped(1)
    gather_own(0, 1)
    put_out(wq, wall, mycols, 0)
    put(chosen, lprev, wx_s.at[3], wx_r.at[3], (znext, t))
    put(stream, bulk, wx_s.at[4], wx_r.at[4], (znext, t))
    order_vectors()
    gather_group(0, 0)
    gather_group(0, 1)
    place_kv()
    put_out(w2o, w2p, slice(None), 1)
    tables(0)
    gather_far(0, 0)
    lay_out(wo, woa, loc.at[4])
    put_out(wo, woa, mycols, 2)
    ready_weights()
    near(0, 0)
    gather_far(0, 1)
    near(0, 1)
    rest(0, 0)
    rest(0, 1)
    attend(0, 0)
    attend(0, 1)
    spread(1)
    gather_group(1, 0)
    base_rows()
    gather_group(1, 1)
    base_take(0)
    base_take(1)
    tables(1)
    gather_far(1, 0)
    ready_wo()
    near_out(0, 0)
    gather_far(1, 1)
    near_out(0, 1)
    token_map()
    out_weights(1)
    base_kept(0)
    rest_out(0, 0)
    base_kept(1)
    rest_out(0, 1)
    out_weights(3)
    out_weights(0)
    base_moved(0)
    base_moved(1)
    gather_group(2, 0)
    gather_group(2, 1)
    unlisted(0, 4)
    gather_far(2, 0)
    near(1, 0)
    gather_far(2, 1)
    near(1, 1)
    rest(1, 0)
    rest(1, 1)
    out_weights(2)
    attend(1, 0)
    attend(1, 1)
    unlisted(4, 8)
    ready_ring()
    mix_out(1, 0)
    mix_out(1, 1)
    finish(1, 0)
    finish(1, 1)
    write(0)
    write(1)
    for cp in sends:
        cp.wait_send()


def body(stream, incoming, chosen, live, norm_gain, router, wq, wk, wv, wo):
    half = HD // 2
    freq = np.exp(-math.log(500000.0) * 2.0 * np.arange(half) / HD)
    freq = jnp.asarray(np.concatenate([freq, freq])[None, :], F32)
    vmem = pl.BlockSpec(memory_space=pltpu.VMEM)
    hbm = pl.BlockSpec(memory_space=pl.ANY)
    dma = pltpu.SemaphoreType.DMA
    scratch = [
        pltpu.VMEM((TOKENS, 128), BF16),
        pltpu.VMEM((TOKENS, 128), BF16),
        pltpu.VMEM((TOKENS, 128), BF16),
        pltpu.VMEM((D, 384), BF16),
        pltpu.VMEM((D, 256), BF16),
        pltpu.VMEM((4, 4, 256, 256), BF16),
        pltpu.VMEM((32, D), BF16),
        pltpu.VMEM((32, D), BF16),
        pltpu.VMEM((D, 128), BF16),
        pltpu.VMEM((D, 128), BF16),
        pltpu.VMEM((1, D), F32),
        pltpu.VMEM((1, D), F32),
        pltpu.VMEM((N * H, CAP), BF16),
        pltpu.VMEM((2, CAP), jnp.int32),
        pltpu.VMEM((2, CAP, 128), F32),
        pltpu.VMEM((2, CAP, 128), F32),
        pltpu.VMEM((2, CAP, 128), F32),
        pltpu.VMEM((3, N, 16, H, 256), BF16),
        pltpu.VMEM((N, 4, H, 256), BF16),
        pltpu.VMEM((N, 3, H, 256), BF16),
        pltpu.VMEM((N, 3, H, 256), BF16),
        pltpu.VMEM((2, N, H, 128), BF16),
        pltpu.VMEM((N, H, 256), BF16),
        pltpu.VMEM((2, 2, CAP, 128), BF16),
        pltpu.VMEM((CAP, 128), BF16),
        pltpu.VMEM((CAP, 128), BF16),
        pltpu.VMEM((N, 2 * H, 128), BF16),
        pltpu.VMEM((N, H, 384), F32),
        pltpu.VMEM((N, H, 128), F32),
        pltpu.VMEM((N, H, 128), F32),
        pltpu.VMEM((N, H, 128), F32),
        pltpu.VMEM((N, H, 256), F32),
        pltpu.VMEM((N, H, 256), BF16),
        pltpu.VMEM((N * H, 256), F32),
        pltpu.VMEM((CAP, 256), BF16),
        pltpu.VMEM((N, H, 128), BF16),
        pltpu.VMEM((CAP, 128), BF16),
        pltpu.VMEM((TOKENS, CAP), BF16),
        pltpu.VMEM((TOKENS, 128), F32),
        dma((7,)),
        dma((3, N, 7)),
        dma((3, N, 7)),
        dma((N, 3)),
        dma((N, 3)),
        dma((N, 3)),
        dma((N, 3)),
        dma((4, 2)),
        dma((4, 2)),
        dma((2, N)),
        dma((2, N)),
        dma((2, N, 3)),
        dma((2, N, 3)),
        dma((N, 2)),
        dma((N, 2)),
        dma((5,)),
        dma((5,)),
        dma((N,)),
        dma((N,)),
    ]
    result = pl.pallas_call(
        kernel,
        out_shape=jax.ShapeDtypeStruct((TOKENS, 128), BF16),
        in_specs=[hbm, hbm, vmem, vmem, vmem, vmem, vmem, hbm, hbm, hbm, hbm],
        out_specs=vmem,
        scratch_shapes=scratch,
        compiler_params=pltpu.CompilerParams(
            collective_id=0, has_side_effects=True, vmem_limit_bytes=62 * 2**20
        ),
        name="relay",
    )(stream[0], incoming[0], chosen[0], live, norm_gain, router, freq, wq[0], jnp.swapaxes(wk[0], 0, 1), jnp.swapaxes(wv[0], 0, 1), wo[0])
    return result[None]


def solution(mesh):
    in_specs = (
        P("pipe", None, "tp"),
        P(None, None, "tp"),
        P("pipe", None, None),
        P("pipe", None),
        P("pipe", None),
        P("pipe", None),
        P("pipe", None, "tp"),
        P("pipe", None, "tp"),
        P("pipe", None, "tp"),
        P("pipe", None, "tp"),
    )
    out_specs = P("pipe", None, "tp")
    return jax.shard_map(body, mesh=mesh, in_specs=in_specs, out_specs=out_specs, check_vma=False)
```

```python
import functools
import math

import jax
import jax.numpy as jnp
import numpy as np
from jax import lax
from jax.experimental import pallas as pl
from jax.experimental.pallas import tpu as pltpu
from jax.sharding import PartitionSpec as P

MESH = pl.DeviceIdType.MESH
F32 = jnp.float32
BF16 = jnp.bfloat16

D = 4096
TOKENS = 2048
CAP = 512
HD = 128
N = 2
R = CAP // N
H = R // 2


def kernel(
    stream, incoming, chosen, live, gain, router, freq, wq, wk, wv, wo, out,
    strm, inc, bulk, wall, woa, wod, wkl, wvl, w2o, w2p, gains, routes, same, lprev, lsp, cosb, sinb, gath, att, rss, rsr, pst, bp, kvb, kc, vc,
    qs, accp, ssb, lgb, mixb, accd, ub, accm, u0, u1s, u1, mt, facc,
    loc, ag_s, ag_r, at_s, at_r, rs_s, rs_r, wo_s, wo_r, pk_s, pk_r, kv_s, kv_r, uz_s, uz_r, wx_s, wx_r, e_s, e_r,
):
    z = lax.axis_index("pipe")
    t = lax.axis_index("tp")
    nz = lax.axis_size("pipe")
    c = t % 2
    chip = t // 2
    y = chip % 4
    x = chip // 4
    p = x * (1 - c) + y * c
    q = y * (1 - c) + x * c
    own = q * 4 + p
    partner = (z, chip * 2 + 1 - c)
    par = y % 2
    twin = x * 4 + y + 1 - 2 * par

    def dev(pp, qq):
        xx = pp * (1 - c) + qq * c
        yy = qq * (1 - c) + pp * c
        return (z, (xx * 4 + yy) * 2 + c)

    def cross(pp, qq):
        xx = pp * (1 - c) + qq * c
        yy = qq * (1 - c) + pp * c
        return (z, (xx * 4 + yy) * 2 + 1 - c)

    znext = (z + 1) % nz
    zprev = (z + nz - 1) % nz
    other = chip * 2 + 1 - c

    barrier = pltpu.get_barrier_semaphore()
    peers = [dev((p + d) % 4, q) for d in (1, 2, 3)] + [dev(p, (q + d) % 4) for d in (1, 2, 3)]
    peers += [cross((p + d) % 4, q) for d in (1, 2, 3)] + [cross(p, (q + d) % 4) for d in (1, 2, 3)] + [partner]
    peers += [(znext, t), (znext, other), (zprev, t), (zprev, other)]
    for peer in peers:
        pl.semaphore_signal(barrier, inc=1, device_id=peer, device_id_type=MESH)

    sends = []

    def put(src, dst, s_sem, r_sem, device):
        cp = pltpu.make_async_remote_copy(
            src_ref=src, dst_ref=dst, send_sem=s_sem, recv_sem=r_sem, device_id=device, device_id_type=MESH
        )
        cp.start()
        sends.append(cp)

    def got(dst, s_sem, r_sem):
        pltpu.make_async_remote_copy(
            src_ref=dst, dst_ref=dst, send_sem=s_sem, recv_sem=r_sem, device_id=partner, device_id_type=MESH
        ).wait_recv()

    mycols = pl.ds(pl.multiple_of(c * 128, 128), 128)

    def local(k, src, dst):
        cp = pltpu.make_async_copy(src, dst, loc.at[k])
        cp.start()
        return cp

    cp_strm = local(0, stream, strm)
    cp_wk = local(1, wk, wkl)
    cp_wv = local(2, wv, wvl)
    cp_inc = local(5, incoming, inc)

    def slot_of(k, cc):
        return ((k % 4) * 4 + k // 4) * (1 - cc) + k * cc

    def part(k):
        return pl.ds(pl.multiple_of(k * 256, 256), 256)

    def lay_out(source, target, sem):
        def some(k, _):
            pltpu.make_async_copy(source.at[part(k), :], target.at[part(slot_of(k, c)), mycols], sem).start()
            return 0

        lax.fori_loop(0, 16, some, 0)

    lay_out(wq, wall, loc.at[3])

    def put_out(source, target, columns, k):
        def some(i, _):
            pltpu.make_async_remote_copy(
                src_ref=source.at[part(i), :], dst_ref=target.at[part(slot_of(i, 1 - c)), columns],
                send_sem=wx_s.at[k], recv_sem=wx_r.at[k], device_id=partner, device_id_type=MESH,
            ).start()
            return 0

        lax.fori_loop(0, 16, some, 0)
        whole = target.at[:, columns]
        sends.append(
            pltpu.make_async_remote_copy(
                src_ref=whole, dst_ref=whole, send_sem=wx_s.at[k], recv_sem=wx_r.at[k],
                device_id=partner, device_id_type=MESH,
            )
        )

    def chip_of(pp, qq, cc):
        return (pp * 4 + qq) * (1 - cc) + (qq * 4 + pp) * cc

    def out_weights(d):
        qq = (q + d) % 4
        pp = (p + d) % 4
        for k in range(4):
            if d == 0:
                pltpu.make_async_copy(wo.at[part(chip_of(k, qq, c)), :], wod.at[q, k, :, mycols], loc.at[6]).start()
            else:
                pltpu.make_async_remote_copy(
                    src_ref=wo.at[part(chip_of(k, qq, c)), :], dst_ref=wod.at[q, k, :, mycols],
                    send_sem=wo_s.at[d, 0], recv_sem=wo_r.at[d, 0], device_id=dev(p, qq), device_id_type=MESH,
                ).start()
            pltpu.make_async_remote_copy(
                src_ref=wo.at[part(chip_of(k, pp, 1 - c)), :], dst_ref=wod.at[p, k, :, mycols],
                send_sem=wo_s.at[d, 1], recv_sem=wo_r.at[d, 1], device_id=cross(pp, q), device_id_type=MESH,
            ).start()
        for way in range(2):
            if d or way:
                whole = wod.at[0, :, :, mycols]
                sends.append(
                    pltpu.make_async_remote_copy(
                        src_ref=whole, dst_ref=whole, send_sem=wo_s.at[d, way], recv_sem=wo_r.at[d, way],
                        device_id=partner, device_id_type=MESH,
                    )
                )

    theircols = pl.ds(pl.multiple_of((1 - c) * 128, 128), 128)
    zf = jnp.minimum(z, 1).astype(F32)
    cf = c.astype(F32)

    def rows(g):
        return pl.ds(pl.multiple_of(g * R + c * H, H), H)

    def other_rows(g):
        return pl.ds(pl.multiple_of(g * R + (1 - c) * H, H), H)

    def spread(tick):
        row = chosen[tick : tick + 1, :].astype(F32)
        for k in range(CAP // 128):
            lsp[tick, k * 128 : (k + 1) * 128, :] = jnp.transpose(
                jnp.broadcast_to(row[:, k * 128 : (k + 1) * 128], (128, 128))
            )

    def take_rows(tick, g, source):
        lane = lax.broadcasted_iota(jnp.int32, (R, 256), 1).astype(F32)
        pos = lsp[tick, g * R : (g + 1) * R, :]
        pos = jnp.concatenate([pos, pos], axis=1)
        total = jnp.zeros((R, 128), F32)
        for k in range(TOKENS // 256):
            hot = jnp.where(pos == lane + float(k * 256), 1.0, 0.0).astype(BF16)
            total += jnp.dot(hot, source(k), preferred_element_type=F32)
        return total

    def mine_of(value):
        low, high = value[:H], value[H:]
        return (low * (1 - cf) + high * cf).astype(BF16), (high * (1 - cf) + low * cf).astype(BF16)

    def pass_on(a, g, block):
        for k, d in ((3, 1), (4, 3)):
            pltpu.make_async_remote_copy(
                src_ref=gath.at[a, g, block], dst_ref=gath.at[a, g, block], send_sem=ag_s.at[a, g, k],
                recv_sem=ag_r.at[a, g, k], device_id=dev(p, (q + d) % 4), device_id_type=MESH,
            ).start()

    def gather_own(a, g):
        for k, d in ((2, 2), (0, 1), (1, 3)):
            put(gath.at[a, g, own], gath.at[a, g, own], ag_s.at[a, g, k], ag_r.at[a, g, k], dev((p + d) % 4, q))
        pass_on(a, g, own)

    def group(qq):
        return pl.ds(qq * 4, 4)

    def gather_group(a, g):
        for k, d in enumerate((1, 3, 2)):
            block = q * 4 + (p + 4 - d) % 4
            got(gath.at[a, g, block], ag_s.at[a, g, k], ag_r.at[a, g, k])
            pass_on(a, g, block)
        for k in (3, 4):
            mine = gath.at[a, g, group(q)]
            sends.append(
                pltpu.make_async_remote_copy(
                    src_ref=mine, dst_ref=mine, send_sem=ag_s.at[a, g, k], recv_sem=ag_r.at[a, g, k],
                    device_id=partner, device_id_type=MESH,
                )
            )

    def gather_far(a, g):
        before = (q + 3) % 4
        after = (q + 1) % 4
        got(gath.at[a, g, group(before)], ag_s.at[a, g, 3], ag_r.at[a, g, 3])
        half = gath.at[a, g, pl.ds(before * 4, 2)]
        put(half, half, ag_s.at[a, g, 5], ag_r.at[a, g, 5], dev(p, after))
        got(gath.at[a, g, group(after)], ag_s.at[a, g, 4], ag_r.at[a, g, 4])
        half = gath.at[a, g, pl.ds(after * 4 + 2, 2)]
        put(half, half, ag_s.at[a, g, 6], ag_r.at[a, g, 6], dev(p, before))

    def gather_end(a, g):
        far = (q + 2) % 4
        got(gath.at[a, g, pl.ds(far * 4, 2)], ag_s.at[a, g, 5], ag_r.at[a, g, 5])
        got(gath.at[a, g, pl.ds(far * 4 + 2, 2)], ag_s.at[a, g, 6], ag_r.at[a, g, 6])

    def features(slot):
        return ((slot % 4) * 4 + slot // 4) * (1 - c) + slot * c

    def order_vectors():
        for k in range(16):
            at = part(features(k))
            gains[:, k * 256 : (k + 1) * 256] = gain[:, at]
            routes[:, k * 256 : (k + 1) * 256] = router[:, at].astype(F32)

    def project(tick, g, shifts, first):
        sums = jnp.zeros((H, 384), F32) if first else accp[g]
        square = jnp.zeros((H, 128), F32) if first else ssb[g]
        logit = jnp.zeros((H, 128), F32) if first else lgb[g]
        for shift in shifts:
            qq = (q + shift) % 4
            for pp in range(4):
                slot = qq * 4 + pp
                wide = gath[2 * tick, g, slot].astype(F32)
                scaled = (wide * gains[:, part(slot)]).astype(BF16)
                two = wide * wide
                square += two[:, :128] + two[:, 128:]
                two = scaled.astype(F32) * routes[:, part(slot)]
                logit += two[:, :128] + two[:, 128:]
                sums += jnp.dot(scaled, wall[part(slot), :], preferred_element_type=F32)
        return sums, square, logit

    def near(tick, g):
        accp[g], ssb[g], lgb[g] = project(tick, g, (0, 3, 1), True)

    def rope(value, cosine, sine):
        return value * cosine + pltpu.roll(value, 64, 1) * sine

    def rest(tick, g):
        gather_end(2 * tick, g)
        sums, square, logit = project(tick, g, (2,), False)
        rstd = lax.rsqrt(jnp.sum(square, axis=1, keepdims=True) / D + 1e-05)
        kv = (sums[:, 256:] * rstd).astype(BF16)
        kvb[tick, par, rows(g), :] = kv
        mine = kvb.at[tick, par, rows(g), :]
        put(mine, mine, kv_s.at[tick, g, 0], kv_r.at[tick, g, 0], (z, twin * 2 + c))
        put(mine, mine, kv_s.at[tick, g, 1], kv_r.at[tick, g, 1], (z, twin * 2 + 1 - c))
        put(mine, mine, kv_s.at[tick, g, 2], kv_r.at[tick, g, 2], partner)
        cosine = cosb[tick, rows(g), :]
        sine = sinb[tick, rows(g), :]
        query = sums * rstd
        qs[g, :H, :] = rope(query[:, :128], cosine, sine).astype(BF16)
        qs[g, H:, :] = rope(query[:, 128:256], cosine, sine).astype(BF16)
        logit = jnp.sum(logit, axis=1, keepdims=True) * rstd
        slot = lax.broadcasted_iota(jnp.int32, (H, 1), 0) + (g * R + c * H)
        alive = jnp.where(slot < live[:, tick : tick + 1], 1.0, 0.0)
        mixb[g] = jnp.broadcast_to(jax.nn.sigmoid(logit) * alive, (H, 128))

    def attend(tick, g):
        got(kvb.at[tick, 1 - par, rows(g), :], kv_s.at[tick, g, 0], kv_r.at[tick, g, 0])
        got(kvb.at[tick, 1 - par, other_rows(g), :], kv_s.at[tick, g, 1], kv_r.at[tick, g, 1])
        got(kvb.at[tick, par, other_rows(g), :], kv_s.at[tick, g, 2], kv_r.at[tick, g, 2])
        span = slice(g * R, (g + 1) * R)
        low = kvb[tick, 0, span, :].astype(F32)
        high = kvb[tick, 1, span, :].astype(F32)
        left = lax.broadcasted_iota(jnp.int32, (R, 128), 1) < 64
        key = jnp.where(left, low, pltpu.roll(high, 64, 1))
        kc[span, :] = rope(key, cosb[tick, span, :], sinb[tick, span, :]).astype(BF16)
        vc[span, :] = jnp.where(left, pltpu.roll(low, 64, 1), high).astype(BF16)
        upto = (g + 1) * R
        scores = lax.dot_general(
            qs[g], kc[:upto, :], (((1,), (1,)), ((), ())), preferred_element_type=F32
        ) * (1.0 / math.sqrt(HD))
        row = lax.broadcasted_iota(jnp.int32, (2 * H, upto), 0)
        row = jnp.where(row < H, row, row - H) + (g * R + c * H)
        col = lax.broadcasted_iota(jnp.int32, (2 * H, upto), 1)
        scores = jnp.where((col <= row) & (col < live[:, tick : tick + 1]), scores, -jnp.inf)
        top = jnp.max(scores, axis=1, keepdims=True)
        weights = jnp.exp(scores - top)
        probs = (weights / jnp.sum(weights, axis=1, keepdims=True)).astype(BF16)
        result = jnp.dot(probs, vc[:upto, :], preferred_element_type=F32).astype(BF16)
        if tick == 0:
            gath[1, g, own, :, 0:128] = result[:H]
            gath[1, g, own, :, 128:256] = result[H:]
            gather_own(1, g)
        else:
            att[g, p, :, 0:128] = result[:H]
            att[g, p, :, 128:256] = result[H:]
            mine = att.at[g, p]
            for k, d in ((2, 2), (0, 1), (1, 3)):
                put(mine, mine, at_s.at[g, k], at_r.at[g, k], dev((p + d) % 4, q))

    def out_part(g, shifts, first):
        total = jnp.zeros((H, 256), F32) if first else accd[g]
        for shift in shifts:
            qq = (q + shift) % 4
            for pp in range(4):
                slot = qq * 4 + pp
                total += jnp.dot(gath[1, g, slot], woa[part(slot), :], preferred_element_type=F32)
        return total

    def near_out(tick, g):
        accd[g] = out_part(g, (0, 3, 1), True)

    def mix_out(tick, g):
        for k, d in enumerate((1, 3, 2)):
            got(att.at[g, (p + 4 - d) % 4], at_s.at[g, k], at_r.at[g, k])
        for d in (2, 1, 3, 0):
            qq = (q + d) % 4
            total = jnp.zeros((H, 256), F32)
            for pp in range(4):
                total += jnp.dot(att[g, pp], wod[qq, pp], preferred_element_type=F32)
            if d == 0:
                accd[g] = total
            else:
                rss[g, d - 1] = total.astype(BF16)
                put(
                    rss.at[g, d - 1], rsr.at[g, d - 1], rs_s.at[g, d - 1], rs_r.at[g, d - 1],
                    dev(p, qq),
                )

    def rest_out(tick, g):
        gather_end(2 * tick + 1, g)
        delta = out_part(g, (2,), False)
        update(tick, g, delta)

    def finish(tick, g):
        delta = accd[g]
        for d in (1, 3, 2):
            got(rsr.at[g, d - 1], rs_s.at[g, d - 1], rs_r.at[g, d - 1])
            delta += rsr[g, d - 1].astype(F32)
        update(tick, g, delta)

    def update(tick, g, delta):
        mixing = jnp.concatenate([mixb[g], mixb[g]], axis=1)
        new = (gath[2 * tick, g, own].astype(F32) + mixing * delta).astype(BF16)
        if tick == 0:
            ub[g] = new
            put(ub.at[g], u0.at[rows(g), :], uz_s.at[g, 0], uz_r.at[g, 0], (znext, t))
            put(ub.at[g], u0.at[rows(g), :], uz_s.at[g, 1], uz_r.at[g, 1], (znext, other))
        else:
            low, high = new[:, :128].astype(F32), new[:, 128:].astype(F32)
            u1s[g] = (high * (1 - cf) + low * cf).astype(BF16)
            put(u1s.at[g], u1.at[rows(g), :], e_s.at[g], e_r.at[g], partner)
            u1[rows(g), :] = (low * (1 - cf) + high * cf).astype(BF16)

    def tables(tick):
        for g in range(CAP // 128):
            span = slice(g * 128, (g + 1) * 128)
            angle = lsp[tick, span, :] * freq[...]
            sign = jnp.where(lax.broadcasted_iota(jnp.int32, (128, 128), 1) < 64, -1.0, 1.0)
            cosb[tick, span, :] = jnp.cos(angle)
            sinb[tick, span, :] = jnp.sin(angle) * sign

    def place_kv():
        cp_wk.wait()
        cp_wv.wait()
        row = lax.broadcasted_iota(jnp.int32, (64, 128), 0)
        col = lax.broadcasted_iota(jnp.int32, (64, 128), 1)
        row = jnp.where(row < 32, row, row + 32) + 32 * c
        hot = jnp.where(col == row, 1.0, 0.0).astype(BF16)

        def some(k, _):
            at = pl.ds(pl.multiple_of(k * 512, 512), 512)
            both = jnp.concatenate([wkl[:, at], wvl[:, at]], axis=0)
            w2o[at, :] = lax.dot_general(both, hot, (((0,), (0,)), ((), ())), preferred_element_type=F32).astype(BF16)
            return 0

        lax.fori_loop(0, D // 512, some, 0)

    def ready_weights():
        pltpu.make_async_copy(wq, wall.at[:, mycols], loc.at[3]).wait()
        got(wall.at[:, theircols], wx_s.at[0], wx_r.at[0])
        got(w2p, wx_s.at[1], wx_r.at[1])

        def some(k, _):
            wall[part(k), 256:] = w2o[part(features(k)), :] + w2p[part(k), :]
            return 0

        lax.fori_loop(0, 16, some, 0)

    def ready_wo():
        pltpu.make_async_copy(wo, woa.at[:, mycols], loc.at[4]).wait()
        got(woa.at[:, theircols], wx_s.at[2], wx_r.at[2])

    def ready_ring():
        pltpu.make_async_copy(wod.at[q, :, :, mycols], wod.at[q, :, :, mycols], loc.at[6]).wait()
        got(wod.at[q, :, :, theircols], wo_s.at[0, 1], wo_r.at[0, 1])
        for d in (1, 3, 2):
            from_q = (q + 4 - d) % 4
            got(wod.at[from_q, :, :, mycols], wo_s.at[d, 0], wo_r.at[d, 0])
            got(wod.at[from_q, :, :, theircols], wo_s.at[d, 1], wo_r.at[d, 1])

    def token_map():
        row = chosen[1:2, :].astype(F32)

        def some(k, _):
            token = (lax.broadcasted_iota(jnp.int32, (256, CAP), 0) + k * 256).astype(F32)
            hot = jnp.where(token == row, 1.0, 0.0).astype(BF16)
            mt[part(k), :] = hot
            facc[part(k), :] = 1.0 - jnp.dot(hot, jnp.ones((CAP, 128), BF16), preferred_element_type=F32)
            return 0

        lax.fori_loop(0, TOKENS // 256, some, 0)

    def base_rows():
        cp_inc.wait()
        got(bulk, wx_s.at[4], wx_r.at[4])
        got(lprev, wx_s.at[3], wx_r.at[3])

        def some(k, _):
            mixed = bulk[part(k), :].astype(F32) * zf + inc[part(k), :].astype(F32) * (1 - zf)
            strm[part(k), :] = mixed.astype(BF16)
            return 0

        lax.fori_loop(0, TOKENS // 256, some, 0)

    def base_take(g):
        mine, others = mine_of(take_rows(1, g, lambda k: strm[k * 256 : (k + 1) * 256, :]))
        bp[g, :, mycols] = mine
        pst[1, g] = others
        put(pst.at[1, g], bp.at[g, :, mycols], pk_s.at[1, g], pk_r.at[1, g], partner)

    def previous():
        return lprev[0:1, :].astype(F32) * zf - (1 - zf)

    def base_kept(g):
        got(bp.at[g, :, theircols], pk_s.at[1, g], pk_r.at[1, g])
        pos = lsp[1, rows(g), :]
        pos = jnp.concatenate([pos] * (CAP // 128), axis=1)
        hot = jnp.where(pos == previous(), 1.0, 0.0)
        same[g * H : (g + 1) * H, :] = hot.astype(BF16)
        accm[g * H : (g + 1) * H, :] = bp[g].astype(F32) * (1.0 - jnp.sum(hot, axis=1, keepdims=True))

    def base_moved(g):
        got(u0.at[rows(g), :], uz_s.at[g, 0], uz_r.at[g, 0])
        got(u0.at[other_rows(g), :], uz_s.at[g, 1], uz_r.at[g, 1])
        span = slice(g * R, (g + 1) * R)
        total = accm[...] + jnp.dot(same[:, span], u0[span, :], preferred_element_type=F32)
        if g < N - 1:
            accm[...] = total
        else:
            for k in range(N):
                gath[2, k, own] = total[k * H : (k + 1) * H].astype(BF16)
                gather_own(2, k)

    def unlisted(first, last):
        both = jnp.concatenate([u0[:, mycols], jnp.ones((CAP, 128), BF16)], axis=1)
        row = previous()

        def some(k, _):
            token = (lax.broadcasted_iota(jnp.int32, (256, CAP), 0) + k * 256).astype(F32)
            hot = jnp.where(token == row, 1.0, 0.0).astype(BF16)
            moved = jnp.dot(hot, both, preferred_element_type=F32)
            state = strm[part(k), :].astype(F32) * (1.0 - moved[:, 128:]) + moved[:, :128]
            facc[part(k), :] = state * facc[part(k), :]
            return 0

        lax.fori_loop(first, last, some, 0)

    def write(g):
        got(u1.at[other_rows(g), :], e_s.at[g], e_r.at[g])
        span = slice(g * R, (g + 1) * R)

        def some(k, _):
            total = facc[part(k), :] + jnp.dot(mt[part(k), span], u1[span, :], preferred_element_type=F32)
            if g < N - 1:
                facc[part(k), :] = total
            else:
                out[part(k), :] = total.astype(BF16)
            return 0

        lax.fori_loop(0, TOKENS // 256, some, 0)

    def pick(g):
        mine, others = mine_of(take_rows(0, g, lambda k: strm[k * 256 : (k + 1) * 256, :]))
        gath[0, g, own, :, mycols] = mine
        pst[0, g] = others

    def swap(g):
        put(pst.at[0, g], gath.at[0, g, p * 4 + q, :, mycols], pk_s.at[0, g], pk_r.at[0, g], partner)

    def swapped(g):
        got(gath.at[0, g, own, :, theircols], pk_s.at[0, g], pk_r.at[0, g])

    spread(0)
    cp_strm.wait()
    pick(0)
    pl.semaphore_wait(barrier, len(peers))
    swap(0)
    pick(1)
    swap(1)
    swapped(0)
    gather_own(0, 0)
    swapped(1)
    gather_own(0, 1)
    put_out(wq, wall, mycols, 0)
    put(chosen, lprev, wx_s.at[3], wx_r.at[3], (znext, t))
    put(stream, bulk, wx_s.at[4], wx_r.at[4], (znext, t))
    order_vectors()
    gather_group(0, 0)
    gather_group(0, 1)
    place_kv()
    put_out(w2o, w2p, slice(None), 1)
    tables(0)
    gather_far(0, 0)
    lay_out(wo, woa, loc.at[4])
    put_out(wo, woa, mycols, 2)
    ready_weights()
    near(0, 0)
    gather_far(0, 1)
    near(0, 1)
    rest(0, 0)
    rest(0, 1)
    attend(0, 0)
    attend(0, 1)
    spread(1)
    gather_group(1, 0)
    base_rows()
    gather_group(1, 1)
    base_take(0)
    base_take(1)
    tables(1)
    gather_far(1, 0)
    ready_wo()
    near_out(0, 0)
    gather_far(1, 1)
    near_out(0, 1)
    token_map()
    out_weights(1)
    base_kept(0)
    rest_out(0, 0)
    base_kept(1)
    rest_out(0, 1)
    out_weights(3)
    out_weights(0)
    base_moved(0)
    base_moved(1)
    gather_group(2, 0)
    gather_group(2, 1)
    unlisted(0, 4)
    gather_far(2, 0)
    near(1, 0)
    gather_far(2, 1)
    near(1, 1)
    rest(1, 0)
    rest(1, 1)
    out_weights(2)
    attend(1, 0)
    attend(1, 1)
    unlisted(4, 8)
    ready_ring()
    mix_out(1, 0)
    mix_out(1, 1)
    finish(1, 0)
    finish(1, 1)
    write(0)
    write(1)
    for cp in sends:
        cp.wait_send()


def body(stream, incoming, chosen, live, norm_gain, router, wq, wk, wv, wo):
    half = HD // 2
    freq = np.exp(-math.log(500000.0) * 2.0 * np.arange(half) / HD)
    freq = jnp.asarray(np.concatenate([freq, freq])[None, :], F32)
    vmem = pl.BlockSpec(memory_space=pltpu.VMEM)
    hbm = pl.BlockSpec(memory_space=pl.ANY)
    dma = pltpu.SemaphoreType.DMA
    scratch = [
        pltpu.VMEM((TOKENS, 128), BF16),
        pltpu.VMEM((TOKENS, 128), BF16),
        pltpu.VMEM((TOKENS, 128), BF16),
        pltpu.VMEM((D, 384), BF16),
        pltpu.VMEM((D, 256), BF16),
        pltpu.VMEM((4, 4, 256, 256), BF16),
        pltpu.VMEM((32, D), BF16),
        pltpu.VMEM((32, D), BF16),
        pltpu.VMEM((D, 128), BF16),
        pltpu.VMEM((D, 128), BF16),
        pltpu.VMEM((1, D), F32),
        pltpu.VMEM((1, D), F32),
        pltpu.VMEM((N * H, CAP), BF16),
        pltpu.VMEM((2, CAP), jnp.int32),
        pltpu.VMEM((2, CAP, 128), F32),
        pltpu.VMEM((2, CAP, 128), F32),
        pltpu.VMEM((2, CAP, 128), F32),
        pltpu.VMEM((3, N, 16, H, 256), BF16),
        pltpu.VMEM((N, 4, H, 256), BF16),
        pltpu.VMEM((N, 3, H, 256), BF16),
        pltpu.VMEM((N, 3, H, 256), BF16),
        pltpu.VMEM((2, N, H, 128), BF16),
        pltpu.VMEM((N, H, 256), BF16),
        pltpu.VMEM((2, 2, CAP, 128), BF16),
        pltpu.VMEM((CAP, 128), BF16),
        pltpu.VMEM((CAP, 128), BF16),
        pltpu.VMEM((N, 2 * H, 128), BF16),
        pltpu.VMEM((N, H, 384), F32),
        pltpu.VMEM((N, H, 128), F32),
        pltpu.VMEM((N, H, 128), F32),
        pltpu.VMEM((N, H, 128), F32),
        pltpu.VMEM((N, H, 256), F32),
        pltpu.VMEM((N, H, 256), BF16),
        pltpu.VMEM((N * H, 256), F32),
        pltpu.VMEM((CAP, 256), BF16),
        pltpu.VMEM((N, H, 128), BF16),
        pltpu.VMEM((CAP, 128), BF16),
        pltpu.VMEM((TOKENS, CAP), BF16),
        pltpu.VMEM((TOKENS, 128), F32),
        dma((7,)),
        dma((3, N, 7)),
        dma((3, N, 7)),
        dma((N, 3)),
        dma((N, 3)),
        dma((N, 3)),
        dma((N, 3)),
        dma((4, 2)),
        dma((4, 2)),
        dma((2, N)),
        dma((2, N)),
        dma((2, N, 3)),
        dma((2, N, 3)),
        dma((N, 2)),
        dma((N, 2)),
        dma((5,)),
        dma((5,)),
        dma((N,)),
        dma((N,)),
    ]
    result = pl.pallas_call(
        kernel,
        out_shape=jax.ShapeDtypeStruct((TOKENS, 128), BF16),
        in_specs=[hbm, hbm, vmem, vmem, vmem, vmem, vmem, hbm, hbm, hbm, hbm],
        out_specs=vmem,
        scratch_shapes=scratch,
        compiler_params=pltpu.CompilerParams(
            collective_id=0, has_side_effects=True, vmem_limit_bytes=62 * 2**20
        ),
        name="relay",
    )(stream[0], incoming[0], chosen[0], live, norm_gain, router, freq, wq[0], jnp.swapaxes(wk[0], 0, 1), jnp.swapaxes(wv[0], 0, 1), wo[0])
    return result[None]


def solution(mesh):
    in_specs = (
        P("pipe", None, "tp"),
        P(None, None, "tp"),
        P("pipe", None, None),
        P("pipe", None),
        P("pipe", None),
        P("pipe", None),
        P("pipe", None, "tp"),
        P("pipe", None, "tp"),
        P("pipe", None, "tp"),
        P("pipe", None, "tp"),
    )
    out_specs = P("pipe", None, "tp")
    return jax.shard_map(body, mesh=mesh, in_specs=in_specs, out_specs=out_specs, check_vma=False)
```
